128 devices in a mesh: section: 2 (over x_lo), cache: 16 (over y, x_hi, core), mp: 4 (over z).
Axes of the slice: x: 4 (x_hi: 2, x_lo: 2; x = x_hi * 2 + x_lo), y: 4, z: 4, core: 2. Of those that a mesh axis runs over, the one named last changes fastest.
Arguments:
- x_in: bfloat16 [16, 2048, 8192], P('cache', 'section', 'mp'), may hold values from -6 to 6
- z_in: bfloat16 [16, 2048, 8192], P('cache', 'section', 'mp'), may hold values from -6 to 6
- bc_in: bfloat16 [16, 2048, 8, 256], P('cache', 'section', 'mp'), may hold values from -6 to 6
- dt_in: bfloat16 [16, 2048, 128], P('cache', 'section', 'mp'), may hold values from -4 to 4
- tail_x: bfloat16 [16, 3, 8192], P('cache', None, 'mp'), may hold values from -6 to 6
- tail_bc: bfloat16 [16, 3, 8, 256], P('cache', None, 'mp'), may hold values from -6 to 6
- conv_w_x: float32 [4, 8192], P(None, 'mp'), may hold values from -3 to 3
- conv_b_x: float32 [8192], P('mp'), may hold values from -3 to 3
- conv_w_bc: float32 [4, 8, 256], P(None, 'mp'), may hold values from -3 to 3
- conv_b_bc: float32 [8, 256], P('mp'), may hold values from -3 to 3
- dt_bias: float32 [128], P('mp'), may hold values from -1 to 1
- decay_rate: float32 [128], P('mp'), may hold values from 0.00024414062 to 0.0234375
- norm_gain: float32 [8192], P('mp'), may hold values from 0.5 to 1.5
- state_pool: float32 [16384, 64, 128], P(('section', 'cache', 'mp')), may hold values from -48 to 48
- block_slots: int32 [16, 128], replicated, may hold values from 0 to 16383, as said below
- new_len: int32 [16], P('cache'), may hold values from 512 to 2048, as said below
Outputs:
- gated_out: bfloat16 [16, 2048, 8192], P('cache', 'section', 'mp')
- final_state: float32 [16, 4, 2, 16, 64, 128], P('cache', 'mp', 'section')
The draws below stay inside these ranges and needn't reach their ends.
Inputs may be any that keep to these rules, and one draw needn't show every extreme that they name: `block_slots`: entry [r, h] is the slot of state_pool holding request r's cached state of head h; all entries differ. That slot lies on a device of section index (h mod (32)) // 16. Of the cached states that one section index needs for the requests of one cache index and the heads of one mp index, at most 2 lie on one device, and in each such set some device holds exactly 2. Positions from new_len[r] on are padding; some request fills all 2048 positions.
All inputs are finite; a program needn't handle non-finite values.
Results may differ from the reference program's by a relative error of at most 0.0085.
Values may be sent and summed in bfloat16 or wider, within the bound.
No kernel may reach another device: no remote copies, remote signals or barrier semaphores. Data moves between devices by JAX's collectives and lax.ppermute only.
A program may use at most 128 MiB of HBM per device.

```python
import math
import jax
import jax.numpy as jnp
from jax import lax

HEADS = 128
HD = 64
DSTATE = 128
NGROUPS = 8
KCONV = 4
BLK = 128
REQ_DEV = 1
DINNER = 8192
REQS = 16
SPAN = 2048
QH = 16
HALVES = 4
QUARTERS = 2
MOST = 2
SLOTS_DEV = 128
POOL = 16384
N_SECTION = 2
N_CACHE = 16
N_MP = 4


def draw_block_slots(key, part):
    key = jax.random.fold_in(key, 11)
    key_hot, key_mix, key_order, key_slot = jax.random.split(key, 4)
    peers = N_CACHE * N_MP
    per_dest = REQ_DEV * QH
    candidate_count = peers * MOST
    planes = N_SECTION * N_CACHE * N_MP
    hot_peer = jax.random.randint(key_hot, (planes,), 0, peers)
    candidates = jnp.arange(candidate_count, dtype=jnp.int32) // MOST
    shuffled = jax.vmap(lambda k: jax.random.permutation(k, candidate_count))(jax.random.split(key_mix, planes))
    owners = candidates[shuffled]
    ranking = jnp.where(owners == hot_peer[:, None], 0, candidate_count) + jnp.arange(candidate_count, dtype=jnp.int32)[None, :]
    ordering = jnp.argsort(ranking, axis=1)
    picked = jnp.take_along_axis(owners, ordering, axis=1)[:, :per_dest]
    mixing = jax.vmap(lambda k: jax.random.permutation(k, per_dest))(jax.random.split(key_order, planes))
    owner_peer = jnp.take_along_axis(picked, mixing, axis=1)
    owner_peer = owner_peer.reshape(N_SECTION, N_CACHE * N_MP * per_dest)
    one_hot = (owner_peer[..., None] == jnp.arange(peers, dtype=jnp.int32)).astype(jnp.int32)
    position = jnp.sum((jnp.cumsum(one_hot, 1) - one_hot) * one_hot, -1)
    slot_perm = jax.vmap(lambda k: jax.random.permutation(k, SLOTS_DEV))(jax.random.split(key_slot, N_SECTION * peers))
    slot_perm = slot_perm.reshape(N_SECTION, peers, SLOTS_DEV)
    local_slot = slot_perm[jnp.arange(N_SECTION, dtype=jnp.int32)[:, None], owner_peer, position]
    global_slot = (jnp.arange(N_SECTION, dtype=jnp.int32)[:, None] * peers + owner_peer) * SLOTS_DEV + local_slot
    global_slot = global_slot.reshape(N_SECTION, N_CACHE, N_MP, REQ_DEV, QH)
    return global_slot.transpose(1, 3, 2, 0, 4).reshape(REQS, N_MP * N_SECTION * QH).astype(jnp.int32)


def draw_new_len(key, part):
    key = jax.random.fold_in(key, 23)
    key_len, key_full = jax.random.split(key)
    lengths = jax.random.randint(key_len, (REQS,), SPAN // 4, SPAN + 1)
    filled = jax.random.randint(key_full, (), 0, REQS)
    return jnp.where(jnp.arange(REQS) == filled, SPAN, lengths).astype(jnp.int32)


def shard_levels(rng, shape, cuts, least, high):
    gain, own = 1.0, jax.random.fold_in(rng, 6)
    for axis_at, parts in cuts:
        steps = jnp.exp(jax.random.uniform(jax.random.fold_in(own, axis_at), (parts,), jnp.float32, least / len(cuts), high / len(cuts)))
        gain = gain * jnp.repeat(steps, shape[axis_at] // parts).reshape([-1 if axis == axis_at else 1 for axis in range(len(shape))])
    return gain


def noise(own_key, dims, spread, limit, shards=(), kind=jnp.bfloat16):
    values = jax.random.normal(own_key, dims, jnp.float32) * spread
    if len(shards) > 0:
        values = shard_levels(own_key, dims, shards, -0.22, 0.18) * values
    return jnp.clip(values, min=-limit, max=limit).astype(kind)


def setup_inputs(seed: int = 0) -> dict:
    key_of = jax.random.split(jax.random.key(seed), 17)
    return {
        "x_in": noise(key_of[0], (REQS, SPAN, DINNER), 1.0, 6.0, ((0, 16), (1, 2), (2, 4))),
        "z_in": noise(key_of[1], (REQS, SPAN, DINNER), 1.0, 6.0, ((0, 16), (1, 2), (2, 4))),
        "bc_in": noise(key_of[2], (REQS, SPAN, NGROUPS, 2 * DSTATE), 1.0, 6.0, ((0, 16), (1, 2), (2, 4))),
        "dt_in": noise(key_of[3], (REQS, SPAN, HEADS), 1.0, 4.0, ((0, 16), (1, 2), (2, 4))),
        "tail_x": noise(key_of[4], (REQS, KCONV - 1, DINNER), 1.0, 6.0, ((0, 16), (2, 4))),
        "tail_bc": noise(key_of[5], (REQS, KCONV - 1, NGROUPS, 2 * DSTATE), 1.0, 6.0, ((0, 16), (2, 4))),
        "conv_w_x": noise(key_of[6], (KCONV, DINNER), KCONV ** -0.5, 3.0, ((1, 4),), jnp.float32),
        "conv_b_x": noise(key_of[7], (DINNER,), 0.5, 3.0, ((0, 4),), jnp.float32),
        "conv_w_bc": noise(key_of[8], (KCONV, NGROUPS, 2 * DSTATE), KCONV ** -0.5, 3.0, ((1, 4),), jnp.float32),
        "conv_b_bc": noise(key_of[9], (NGROUPS, 2 * DSTATE), 0.5, 3.0, ((0, 4),), jnp.float32),
        "dt_bias": jnp.clip(jax.random.uniform(key_of[10], (HEADS,), jnp.float32, -1.0, 1.0) * shard_levels(key_of[10], (HEADS,), ((0, 4),), -0.4, 0.0), -1.0, 1.0),
        "decay_rate": jnp.clip(jnp.exp(math.log(0.0234375) - 4.564348 * jax.random.uniform(key_of[11], (HEADS,), jnp.float32) ** shard_levels(key_of[11], (HEADS,), ((0, 4),), -0.2, 0.2)), 0.00024414062, 0.0234375),
        "norm_gain": jnp.clip(1.0 + 0.1 * jax.random.normal(key_of[12], (DINNER,), jnp.float32), 0.5, 1.5),
        "state_pool": noise(key_of[13], (POOL, HD, DSTATE), 8.0, 48.0, ((0, 128),), jnp.float32),
        "block_slots": draw_block_slots(jax.random.fold_in(key_of[16], 71), 0),
        "new_len": draw_new_len(jax.random.fold_in(key_of[16], 71), 0),
    }


EPS = 1e-05

def conv_part(leading, values, kernel, offset):
    joined = jnp.concatenate([leading, values], 0).astype(jnp.float32)
    length = values.shape[0]
    summed = offset + sum((kernel[k] * joined[k:k + length] for k in range(kernel.shape[0])))
    return jax.nn.silu(summed).astype(jnp.bfloat16)

def reference(x_in, z_in, bc_in, dt_in, tail_x, tail_bc, conv_w_x, conv_b_x, conv_w_bc, conv_b_bc, dt_bias, decay_rate, norm_gain, state_pool, block_slots, new_len):
    per_group = HEADS // NGROUPS
    block_count = SPAN // BLK
    causal = jnp.arange(BLK)[:, None] >= jnp.arange(BLK)[None, :]

    def block_step(carried, pieces):
        x_block, b_block, c_block, a_block, dt_block = pieces
        cum_log = jnp.cumsum(a_block, 0)
        scores = jnp.einsum('tgn,sgn->gts', c_block.astype(jnp.float32), b_block.astype(jnp.float32))
        cum_heads = cum_log.transpose(1, 2, 0)
        log_gap = cum_heads[..., :, None] - cum_heads[..., None, :]
        decays = jnp.where(causal, jnp.exp(jnp.where(causal, log_gap, 0.0)), 0.0)
        weights = (scores[:, None] * decays * dt_block.transpose(1, 2, 0)[..., None, :]).astype(jnp.bfloat16)
        weights = lax.optimization_barrier(weights)
        y_intra = jnp.einsum('gkts,sgkp->tgkp', weights.astype(jnp.float32), x_block.astype(jnp.float32))
        start_low = lax.optimization_barrier(carried.astype(jnp.bfloat16))
        y_inter = jnp.exp(cum_log)[..., None] * jnp.einsum('tgn,gkpn->tgkp', c_block.astype(jnp.float32), start_low.astype(jnp.float32))
        tail_weight = jnp.exp(cum_log[-1:] - cum_log) * dt_block
        x_weighted = lax.optimization_barrier((x_block.astype(jnp.float32) * tail_weight[..., None]).astype(jnp.bfloat16))
        contribution = jnp.einsum('sgkp,sgn->gkpn', x_weighted.astype(jnp.float32), b_block.astype(jnp.float32))
        carried = jnp.exp(cum_log[-1])[..., None, None] * carried + contribution
        y_all = y_intra + y_inter
        return (carried, y_all)

    def one_request(request):
        x_conv = conv_part(tail_x[request], x_in[request], conv_w_x, conv_b_x)
        bc_conv = conv_part(tail_bc[request], bc_in[request], conv_w_bc, conv_b_bc)
        live = (jnp.arange(SPAN, dtype=jnp.int32) < new_len[request]).astype(jnp.float32)
        step_size = jax.nn.softplus(dt_in[request].astype(jnp.float32) + dt_bias) * live[:, None]
        log_decay = -step_size * decay_rate
        start_state = state_pool[block_slots[request]].reshape(NGROUPS, per_group, HD, DSTATE)
        pieces = (x_conv.reshape(block_count, BLK, NGROUPS, per_group, HD), bc_conv[..., :DSTATE].reshape(block_count, BLK, NGROUPS, DSTATE), bc_conv[..., DSTATE:].reshape(block_count, BLK, NGROUPS, DSTATE), log_decay.reshape(block_count, BLK, NGROUPS, per_group), step_size.reshape(block_count, BLK, NGROUPS, per_group))
        ending, outputs = lax.scan(block_step, start_state, pieces)
        y_full = outputs.reshape(SPAN, DINNER)
        gated_vals = y_full * jax.nn.silu(z_in[request].astype(jnp.float32))
        grouped = gated_vals.reshape(SPAN, NGROUPS, DINNER // NGROUPS)
        inverse_rms = lax.rsqrt(lax.optimization_barrier(jnp.mean(grouped * grouped, -1, keepdims=True)) + EPS)
        result = (grouped * inverse_rms).reshape(SPAN, DINNER) * norm_gain * live[:, None]
        return (result.astype(jnp.bfloat16), ending.reshape(HALVES, QUARTERS, QH, HD, DSTATE))
    gated_out, final_state = lax.map(one_request, jnp.arange(REQS, dtype=jnp.int32))
    return (gated_out, final_state)
```

```python
import functools

import jax
import jax.numpy as jnp
from jax import lax
from jax.experimental import pallas as pl
from jax.experimental.pallas import tpu as pltpu
from jax.sharding import PartitionSpec as P

BLK = 128
EPS = 1e-05
MIB = 1 << 20
F32 = jnp.float32
BF16 = jnp.bfloat16
SMEM = pltpu.SMEM
VMEM = pltpu.VMEM


def dot(a, b):
    return jnp.dot(a, b, preferred_element_type=F32)


def silu(v):
    half = 0.5 * v
    return half * jnp.tanh(half) + half


def split_two(v):
    high = v.astype(BF16)
    return high, (v - high.astype(F32)).astype(BF16)


def split_three(v):
    high = v.astype(BF16)
    rest = v - high.astype(F32)
    mid = rest.astype(BF16)
    return high, mid, (rest - mid.astype(F32)).astype(BF16)


def iota(shape, dim):
    return lax.broadcasted_iota(jnp.int32, shape, dim)


def pack_kernel(picked_ref, pool_ref, out_ref):
    count = out_ref.shape[0]
    first = pl.program_id(0) * count

    def one(i, carry):
        out_ref[i] = pool_ref[picked_ref[first + i]].astype(BF16)
        return carry

    lax.fori_loop(0, count, one, 0, unroll=8)


def pack(picked, pool):
    count = picked.shape[0]
    steps = 8
    rows = count // steps
    return pl.pallas_call(
        pack_kernel,
        out_shape=jax.ShapeDtypeStruct((count,) + pool.shape[1:], BF16),
        grid=(steps,),
        in_specs=[
            pl.BlockSpec(memory_space=SMEM),
            pl.BlockSpec(pool.shape, lambda i: (0, 0, 0)),
        ],
        out_specs=pl.BlockSpec((rows,) + pool.shape[1:], lambda i: (i, 0, 0)),
        compiler_params=pltpu.CompilerParams(vmem_limit_bytes=16 * MIB),
        cost_estimate=pl.CostEstimate(flops=0, bytes_accessed=6 * MIB, transcendentals=0),
        name="pack_states",
    )(picked, pool)


def select_kernel(index_ref, incoming_ref, out_ref):
    for pair in range(out_ref.shape[1] // BLK):
        two = jnp.concatenate(
            [incoming_ref[index_ref[2 * pair + k]].astype(F32) for k in range(2)], 0
        )
        out_ref[:, pair * BLK : (pair + 1) * BLK] = two.T.astype(BF16)


def select(index, incoming):
    heads = index.shape[0]
    _, head_dim, state_size = incoming.shape
    return pl.pallas_call(
        select_kernel,
        out_shape=jax.ShapeDtypeStruct((state_size, heads * head_dim), BF16),
        in_specs=[pl.BlockSpec(memory_space=SMEM), pl.BlockSpec(memory_space=VMEM)],
        out_specs=pl.BlockSpec(memory_space=VMEM),
        compiler_params=pltpu.CompilerParams(vmem_limit_bytes=16 * MIB),
        cost_estimate=pl.CostEstimate(flops=0, bytes_accessed=3 * MIB, transcendentals=0),
        name="select_states",
    )(index, incoming)


def local_kernel(
    place_ref, x_ref, z_ref, bc_ref, dt_ref, step_ref, halo_ref, taps_ref,
    a_ref, b_ref, c_ref, t_ref,
    spread, factors, behind, state, decay,
    *, groups, blocks, head_dim, head_count,
):
    step = pl.program_id(0)
    channels = x_ref.shape[1]
    width = channels // groups
    lanes = dt_ref.shape[1]
    halves = lanes // BLK
    chunk = 256

    @pl.when(step == 0)
    def _():
        behind[...] = halo_ref[...]
        state[...] = jnp.zeros_like(state)
        decay[...] = jnp.ones_like(decay)
        for at in range(0, channels, BLK):
            shape = (spread.shape[0], BLK)
            head = lax.div(iota(shape, 1) + at, head_dim)
            spread[:, at : at + BLK] = jnp.where(
                (iota(shape, 0) & (head_count - 1)) == head, 1.0, 0.0
            ).astype(BF16)
        value = dt_ref[...].astype(F32) + step_ref[0:1, :]
        soft = jnp.maximum(value, 0.0) + jnp.log1p(jnp.exp(-jnp.abs(value)))
        shape = (BLK, lanes)
        position = place_ref[1] + lax.div(iota(shape, 1), head_count) * BLK + iota(shape, 0)
        steps = jnp.where(position < place_ref[0], soft, 0.0)
        log_decay = -steps * step_ref[1:2, :]
        lower = jnp.where(iota((BLK, BLK), 0) >= iota((BLK, BLK), 1), 1.0, 0.0).astype(BF16)
        cum_log = sum(dot(lower, part) for part in split_three(log_decay))
        both = (jnp.exp(cum_log), steps * jnp.exp(-cum_log))
        for row, full in enumerate(both):
            for part, values in enumerate(split_two(full)):
                for block in range(blocks):
                    per = BLK // head_count
                    piece = values[:, block // per * BLK : (block // per + 1) * BLK].astype(F32)
                    owner = lax.div(iota((BLK, BLK), 1), head_count)
                    factors[
                        block, row * BLK : (row + 1) * BLK, part * BLK : (part + 1) * BLK
                    ] = jnp.where(owner == block % per, piece, 0.0).astype(BF16)

    def conv(source, at, size, base):
        now = source[:, at : at + size].astype(F32)
        cols = slice(base + at, base + at + size)
        joined = jnp.concatenate([behind[:, cols], now], 0)
        total = taps_ref[4:5, cols] + taps_ref[3:4, cols] * now
        for k in range(3):
            total = total + taps_ref[k : k + 1, cols] * joined[5 + k : 5 + k + BLK]
        behind[:, cols] = now[BLK - 8 :]
        return silu(total)

    causal = iota((BLK, BLK), 0) >= iota((BLK, BLK), 1)
    for group in range(groups):
        mixed = conv(bc_ref, group * 2 * BLK, 2 * BLK, channels)
        b_block = mixed[:, :BLK]
        c_block = mixed[:, BLK:].astype(BF16)
        b_turned = b_block.T.astype(BF16)
        c_ref[:, group * BLK : (group + 1) * BLK] = c_block
        scores = jnp.where(causal, dot(c_block, b_turned), 0.0).astype(BF16)
        left = jnp.concatenate([scores, c_block], 1)
        for at in range(group * width, (group + 1) * width, chunk):
            cols = slice(at, at + chunk)
            x_conv = conv(x_ref, at, chunk, 0)
            scale = dot(factors[step], spread[:, cols])
            risen = scale[:BLK]
            inner = (x_conv * scale[BLK:]).astype(BF16)
            before = state[:, cols]
            y_local = risen * dot(left, jnp.concatenate([inner, before.astype(BF16)], 0))
            last = risen[BLK - 1 :]
            state[:, cols] = last * (before + dot(b_turned, inner))
            gate = silu(z_ref[:, cols].astype(F32))
            passed = decay[0:1, cols]
            a_ref[:, cols] = (y_local * gate).astype(BF16)
            b_ref[:, cols] = (risen * passed * gate).astype(BF16)
            decay[0:1, cols] = passed * last

    @pl.when(step == blocks - 1)
    def _():
        t_ref[:BLK] = state[...].astype(BF16)
        parts = split_three(decay[0:1, :])
        row = iota((16, channels), 0)
        stacked = jnp.zeros((16, channels), F32)
        for k, part in enumerate(parts):
            stacked = jnp.where(row == k, part.astype(F32), stacked)
        t_ref[BLK:] = stacked.astype(BF16)


def local_part(place, x, z, bc, dt, step_rows, halo, taps, groups, head_count):
    seg_len, channels = x.shape
    blocks = seg_len // BLK
    body = functools.partial(
        local_kernel, groups=groups, blocks=blocks,
        head_dim=channels // head_count, head_count=head_count,
    )
    by_block = lambda width: pl.BlockSpec((BLK, width), lambda i: (i, 0))
    whole = lambda shape: pl.BlockSpec(shape, lambda i: (0,) * len(shape))
    return pl.pallas_call(
        body,
        out_shape=(
            jax.ShapeDtypeStruct((seg_len, channels), BF16),
            jax.ShapeDtypeStruct((seg_len, channels), BF16),
            jax.ShapeDtypeStruct((seg_len, groups * BLK), BF16),
            jax.ShapeDtypeStruct((BLK + 16, channels), BF16),
        ),
        grid=(blocks,),
        in_specs=[
            pl.BlockSpec(memory_space=SMEM),
            by_block(channels), by_block(channels), by_block(bc.shape[1]),
            whole(dt.shape), whole(step_rows.shape), whole(halo.shape), whole(taps.shape),
        ],
        out_specs=(
            by_block(channels), by_block(channels), by_block(groups * BLK),
            whole((BLK + 16, channels)),
        ),
        scratch_shapes=[
            VMEM((2 * BLK, channels), BF16),
            VMEM((blocks, 2 * BLK, 2 * BLK), BF16),
            VMEM(halo.shape, F32),
            VMEM((BLK, channels), F32),
            VMEM((8, channels), F32),
        ],
        compiler_params=pltpu.CompilerParams(vmem_limit_bytes=32 * MIB),
        cost_estimate=pl.CostEstimate(
            flops=2 * seg_len * channels * 1024, bytes_accessed=20 * MIB,
            transcendentals=2 * seg_len * channels,
        ),
        name="local_blocks",
    )(place, x, z, bc, dt, step_rows, halo, taps)


def join_kernel(
    place_ref, a_ref, b_ref, c_ref, own_ref, other_ref, mine_ref, theirs_ref, gain_ref,
    out_ref, final_ref,
    start, gated,
    *, groups,
):
    step = pl.program_id(0)
    section = place_ref[2]
    width = a_ref.shape[1] // groups
    chunk = 256

    def decay_of(ref, cols):
        rows = ref[BLK : BLK + 16, cols].astype(F32)
        return rows[0:1] + rows[1:2] + rows[2:3]

    @pl.when(step == 0)
    def _():
        for group in range(groups):
            for at in range(0, width, BLK):
                cols = slice(group * width + at, group * width + at + BLK)
                here = slice(at, at + BLK)

                def moved(first, second, cached):
                    middle = decay_of(first, cols) * cached + first[:BLK, cols].astype(F32)
                    return middle, decay_of(second, cols) * middle + second[:BLK, cols].astype(F32)

                @pl.when(section == 0)
                def _():
                    if group == 0:
                        cached = own_ref[:, here].astype(F32)
                        final_ref[here, :] = moved(mine_ref, theirs_ref, cached)[1].T
                        start[:, cols] = own_ref[:, here]
                    else:
                        start[:, cols] = other_ref[:, here]

                @pl.when(section == 1)
                def _():
                    source = own_ref if group == 1 else other_ref
                    middle, end = moved(theirs_ref, mine_ref, source[:, here].astype(F32))
                    start[:, cols] = middle.astype(BF16)
                    if group == 1:
                        final_ref[here, :] = end.T

    position = place_ref[1] + step * BLK + iota((BLK, 1), 0)
    live = (position < place_ref[0]).astype(F32)
    for group in range(groups):
        c_block = c_ref[:, group * BLK : (group + 1) * BLK]
        squares = jnp.zeros((BLK, BLK), F32)
        for at in range(0, width, chunk):
            cols = slice(group * width + at, group * width + at + chunk)
            inter = dot(c_block, start[:, cols])
            value = a_ref[:, cols].astype(F32) + b_ref[:, cols].astype(F32) * inter
            gated[:, at : at + chunk] = value
            square = value * value
            for k in range(chunk // BLK):
                squares = squares + square[:, k * BLK : (k + 1) * BLK]
        mean = jnp.sum(squares, 1, keepdims=True) * (1.0 / width)
        scale = lax.rsqrt(mean + EPS) * live
        for at in range(0, width, chunk):
            cols = slice(group * width + at, group * width + at + chunk)
            out_ref[:, cols] = (
                gated[:, at : at + chunk] * scale * gain_ref[0:1, cols]
            ).astype(BF16)


def join_part(place, a, b, c, own, other, mine, theirs, gain, groups):
    seg_len, channels = a.shape
    by_block = lambda width: pl.BlockSpec((BLK, width), lambda i: (i, 0))
    whole = lambda shape: pl.BlockSpec(shape, lambda i: (0,) * len(shape))
    final_shape = (own.shape[1], own.shape[0])
    return pl.pallas_call(
        functools.partial(join_kernel, groups=groups),
        out_shape=(
            jax.ShapeDtypeStruct((seg_len, channels), BF16),
            jax.ShapeDtypeStruct(final_shape, F32),
        ),
        grid=(seg_len // BLK,),
        in_specs=[
            pl.BlockSpec(memory_space=SMEM),
            by_block(channels), by_block(channels), by_block(c.shape[1]),
            whole(own.shape), whole(other.shape), whole(mine.shape), whole(theirs.shape),
            whole(gain.shape),
        ],
        out_specs=(by_block(channels), whole(final_shape)),
        scratch_shapes=[VMEM((BLK, channels), BF16), VMEM((BLK, channels // groups), F32)],
        compiler_params=pltpu.CompilerParams(vmem_limit_bytes=32 * MIB),
        cost_estimate=pl.CostEstimate(
            flops=2 * seg_len * channels * BLK, bytes_accessed=16 * MIB, transcendentals=0
        ),
        name="join_blocks",
    )(place, a, b, c, own, other, mine, theirs, gain)


def body(
    x_in,
    z_in,
    bc_in,
    dt_in,
    tail_x,
    tail_bc,
    conv_w_x,
    conv_b_x,
    conv_w_bc,
    conv_b_bc,
    dt_bias,
    decay_rate,
    norm_gain,
    state_pool,
    block_slots,
    new_len,
):
    section = lax.axis_index("section")
    section_count = lax.axis_size("section")
    cache_count = lax.axis_size("cache")
    mp_count = lax.axis_size("mp")
    peer_count = cache_count * mp_count
    peer_self = lax.axis_index("cache") * mp_count + lax.axis_index("mp")
    _, seg_len, channels = x_in.shape
    groups = bc_in.shape[2]
    state_size = bc_in.shape[3] // 2
    head_count = dt_in.shape[2]
    head_dim = channels // head_count
    quarter = head_count // section_count
    blocks = seg_len // BLK
    slots_dev = state_pool.shape[0]
    most_held = slots_dev // peer_count
    swap = [(0, 1), (1, 0)]

    listed = block_slots.reshape(cache_count, mp_count, section_count, quarter)
    listed = lax.dynamic_index_in_dim(listed, section, 2, keepdims=False)
    listed = listed.reshape(peer_count, quarter)
    owner = listed // slots_dev % peer_count
    key = jnp.arange(quarter, dtype=jnp.int32)[None, :] * slots_dev + listed % slots_dev
    mine = owner == peer_self
    first = jnp.min(jnp.where(mine, key, quarter * slots_dev), 1) % slots_dev
    last = jnp.max(jnp.where(mine, key, 0), 1) % slots_dev
    picked = jnp.stack([first, last], 1).reshape(peer_count * most_held)
    outgoing = pack(picked, state_pool)
    incoming = lax.all_to_all(
        outgoing.reshape(peer_count, most_held * head_dim, state_size),
        ("cache", "mp"), split_axis=0, concat_axis=0, tiled=True,
    )
    own_owner = lax.dynamic_index_in_dim(owner, peer_self, 0, keepdims=False)
    order = jnp.arange(quarter)
    again = (own_owner[:, None] == own_owner[None, :]) & (order[None, :] < order[:, None])
    index = own_owner * most_held + jnp.any(again, 1).astype(jnp.int32)

    x2, z2, dt2 = x_in[0], z_in[0], dt_in[0]
    bc2 = bc_in[0].reshape(seg_len, groups * 2 * state_size)
    edge = jnp.concatenate(
        [x2[seg_len - 16 :], bc_in[0, seg_len - 16 :].reshape(16, groups * 2 * state_size)], 1
    )
    received = lax.ppermute(edge, "section", [(0, 1)])
    tail = jnp.concatenate([tail_x[0], tail_bc[0].reshape(3, groups * 2 * state_size)], 1)
    halo = jnp.where(section == 0, jnp.pad(tail, ((5, 0), (0, 0))), received[8:]).astype(F32)

    dt_rows = dt2.reshape(blocks, BLK, head_count).transpose(1, 0, 2).reshape(BLK, -1)
    step_rows = jnp.tile(jnp.stack([dt_bias, decay_rate]), (1, blocks))
    taps = jnp.concatenate(
        [
            jnp.concatenate([conv_w_x, conv_w_bc.reshape(4, -1)], 1),
            jnp.concatenate([conv_b_x, conv_b_bc.reshape(-1)])[None],
        ],
        0,
    )
    place = jnp.stack(
        [new_len[0], section.astype(jnp.int32) * seg_len, section.astype(jnp.int32)]
    )
    a, b, c, summary = local_part(
        place, x2, z2, bc2, dt_rows, step_rows, halo, taps, groups, head_count
    )
    theirs = lax.ppermute(summary, "section", swap)

    own = select(index, incoming.reshape(peer_count * most_held, head_dim, state_size))
    other = lax.ppermute(own, "section", swap)
    gated, final = join_part(
        place, a, b, c, own, other, summary, theirs, norm_gain[None], groups
    )
    return (
        gated[None],
        final.reshape(1, 1, 1, quarter, head_dim, state_size),
    )


def solution(mesh):
    in_specs = (
        P("cache", "section", "mp"),
        P("cache", "section", "mp"),
        P("cache", "section", "mp", None),
        P("cache", "section", "mp"),
        P("cache", None, "mp"),
        P("cache", None, "mp", None),
        P(None, "mp"),
        P("mp"),
        P(None, "mp", None),
        P("mp", None),
        P("mp"),
        P("mp"),
        P("mp"),
        P(("section", "cache", "mp"), None, None),
        P(),
        P("cache"),
    )
    out_specs = (P("cache", "section", "mp"), P("cache", "mp", "section", None, None, None))
    return jax.shard_map(body, mesh=mesh, in_specs=in_specs, out_specs=out_specs, check_vma=False)
```

```python
import functools

import jax
import jax.numpy as jnp
from jax import lax
from jax.experimental import pallas as pl
from jax.experimental.pallas import tpu as pltpu
from jax.sharding import PartitionSpec as P

BLK = 128
EPS = 1e-05
JOIN_ROWS = 512
LOCAL_ROWS = 256
MIB = 1 << 20
VMEM_LIMIT = 56 * MIB
F32 = jnp.float32
BF16 = jnp.bfloat16
SMEM = pltpu.SMEM
VMEM = pltpu.VMEM


def dot(a, b):
    return jnp.dot(a, b, preferred_element_type=F32)


def silu(v):
    half = 0.5 * v
    return half * jnp.tanh(half) + half


def split_two(v):
    high = v.astype(BF16)
    return high, (v - high.astype(F32)).astype(BF16)


def split_three(v):
    high = v.astype(BF16)
    rest = v - high.astype(F32)
    mid = rest.astype(BF16)
    return high, mid, (rest - mid.astype(F32)).astype(BF16)


def iota(shape, dim):
    return lax.broadcasted_iota(jnp.int32, shape, dim)


def over(v, power_of_two):
    return lax.shift_right_logical(v, jnp.int32(power_of_two.bit_length() - 1))


def edge_kernel(x_ref, bc_ref, edge_ref):
    width = x_ref.shape[1]
    edge_ref[:, :width] = x_ref[...]
    rows = bc_ref[...].astype(F32)
    for group in range(bc_ref.shape[1]):
        at = width + group * bc_ref.shape[2]
        edge_ref[:, at : at + bc_ref.shape[2]] = rows[:, group, :].astype(BF16)


def edge_of(x, bc):
    last = x.shape[0] // 16 - 1
    edge = (16, x.shape[1] + bc.shape[1] * bc.shape[2])
    return pl.pallas_call(
        edge_kernel,
        out_shape=jax.ShapeDtypeStruct(edge, BF16),
        grid=(1,),
        in_specs=[
            pl.BlockSpec((16, x.shape[1]), lambda i: (last, 0)),
            pl.BlockSpec((16,) + bc.shape[1:], lambda i: (last, 0, 0)),
        ],
        out_specs=pl.BlockSpec(edge, lambda i: (0, 0)),
        compiler_params=pltpu.CompilerParams(vmem_limit_bytes=VMEM_LIMIT),
        cost_estimate=pl.CostEstimate(flops=0, bytes_accessed=MIB // 4, transcendentals=0),
        name="edge_rows",
    )(x, bc)


def pack_kernel(
    slots_ref, pool_hbm, edge_hbm, out_ref,
    pool, keys, keys_smem, pool_sems, keys_sem,
):
    step = pl.program_id(0)
    section_count = lax.axis_size("section")
    mp_count = lax.axis_size("mp")
    peer_count = lax.axis_size("cache") * mp_count
    slots_dev = pool.shape[0]
    count = out_ref.shape[0]
    heads = slots_ref.shape[1]
    share = heads // mp_count
    quarter = share // section_count
    held = slots_dev // peer_count
    section = lax.axis_index("section")

    @pl.when(step == 0)
    def _():
        part = slots_dev // pool_sems.shape[0]
        copies = []
        for k in range(pool_sems.shape[0]):
            rows = pl.ds(k * part, part)
            copies.append(pltpu.make_async_copy(pool_hbm.at[rows], pool.at[rows], pool_sems.at[k]))
        for copy in copies:
            copy.start()
        me = lax.axis_index("cache") * mp_count + lax.axis_index("mp")
        slots = slots_ref[...]
        lane = iota(slots.shape, 1)
        mine = lax.rem(lax.div(slots, slots_dev), peer_count) == me
        key = lane * slots_dev + lax.rem(slots, slots_dev)
        first = jnp.where(mine, key, heads * slots_dev)
        last = jnp.where(mine, key, 0)
        shift = 1
        while shift < quarter:
            first = jnp.minimum(first, pltpu.roll(first, heads - shift, 1))
            last = jnp.maximum(last, pltpu.roll(last, heads - shift, 1))
            shift *= 2
        keys[0] = lax.rem(first, slots_dev)
        keys[1] = lax.rem(last, slots_dev)
        listing = pltpu.make_async_copy(keys, keys_smem, keys_sem)
        listing.start()
        listing.wait()
        for copy in copies:
            copy.wait()

    base = step * (count // held)

    def one(i, carry):
        dest = base + i
        row = lax.div(dest, mp_count)
        col = lax.rem(dest, mp_count) * share + section * quarter
        for k in range(held):
            out_ref[held * i + k] = pool[keys_smem[k, row, col]].astype(BF16)
        return carry

    lax.fori_loop(0, count // held, one, 0, unroll=8)


def pack(slots, pool, edge):
    steps = 4
    count = pool.shape[0] // steps
    return pl.pallas_call(
        pack_kernel,
        out_shape=jax.ShapeDtypeStruct(pool.shape, BF16),
        grid=(steps,),
        in_specs=[
            pl.BlockSpec(slots.shape, lambda i: (0, 0)),
            pl.BlockSpec(memory_space=pl.ANY),
            pl.BlockSpec(memory_space=pl.ANY),
        ],
        out_specs=pl.BlockSpec((count,) + pool.shape[1:], lambda i: (i, 0, 0)),
        scratch_shapes=[
            VMEM(pool.shape, F32),
            VMEM((2,) + slots.shape, jnp.int32),
            SMEM((2,) + slots.shape, jnp.int32),
            pltpu.SemaphoreType.DMA((4,)),
            pltpu.SemaphoreType.DMA,
        ],
        compiler_params=pltpu.CompilerParams(vmem_limit_bytes=VMEM_LIMIT),
        cost_estimate=pl.CostEstimate(flops=0, bytes_accessed=6 * MIB, transcendentals=0),
        name="pack_states",
    )(slots, pool, edge)


def select_kernel(slots_ref, incoming_ref, out_ref, *, slots_dev, held):
    section_count = lax.axis_size("section")
    mp_count = lax.axis_size("mp")
    peer_count = lax.axis_size("cache") * mp_count
    share = slots_ref.shape[1] // mp_count
    quarter = share // section_count
    row = lax.axis_index("cache")
    at = lax.axis_index("mp") * share + lax.axis_index("section") * quarter
    owners, index = [], []
    for h in range(quarter):
        owner = lax.rem(lax.div(slots_ref[row, at + h], slots_dev), peer_count)
        again = jnp.int32(0)
        for earlier in owners:
            again = jnp.where(earlier == owner, 1, again)
        owners.append(owner)
        index.append(owner * held + again)
    for pair in range(quarter // 2):
        two = jnp.concatenate(
            [incoming_ref[index[2 * pair + k]].astype(F32) for k in range(2)], 0
        )
        out_ref[:, pair * BLK : (pair + 1) * BLK] = two.T.astype(BF16)


def select(slots, incoming, quarter, held):
    count, head_dim, state_size = incoming.shape
    return pl.pallas_call(
        functools.partial(select_kernel, slots_dev=count, held=held),
        out_shape=jax.ShapeDtypeStruct((state_size, quarter * head_dim), BF16),
        in_specs=[pl.BlockSpec(memory_space=SMEM), pl.BlockSpec(memory_space=VMEM)],
        out_specs=pl.BlockSpec(memory_space=VMEM),
        compiler_params=pltpu.CompilerParams(vmem_limit_bytes=VMEM_LIMIT),
        cost_estimate=pl.CostEstimate(flops=0, bytes_accessed=3 * MIB, transcendentals=0),
        name="select_states",
    )(slots, incoming)


def local_kernel(
    len_ref, x_ref, z_ref, bc_ref, dt_ref, bias_ref, rate_ref, got_ref,
    tail_x_ref, tail_bc_ref, tap_x_ref, off_x_ref, tap_bc_ref, off_bc_ref, *rest,
    group, blocks, head_dim,
):
    a_ref, b_ref, c_ref, t_ref, spread, factors, behind, state, decay = rest[-9:]
    step = pl.program_id(0)
    width = x_ref.shape[1]
    heads = width // head_dim
    state_size = bc_ref.shape[1] // 2
    per_step = x_ref.shape[0] // BLK
    chunk = 256
    here = slice(group * heads, (group + 1) * heads)

    @pl.when(step == 0)
    def _():
        section = lax.axis_index("section")
        got_x = got_ref[:, group * width : (group + 1) * width].astype(F32)[8:]
        at = lax.axis_size("section") * width + group * 2 * state_size
        got_bc = got_ref[:, at : at + 2 * state_size].astype(F32)[8:]
        behind[:, :width] = got_x
        behind[:, width:] = got_bc

        @pl.when(section == 0)
        def _():
            behind[5:8, :width] = tail_x_ref[:, group * width : (group + 1) * width].astype(F32)
            behind[5:8, width:] = tail_bc_ref[:, group, :].astype(F32)

        state[...] = jnp.zeros_like(state)
        decay[...] = jnp.ones_like(decay)
        for at in range(0, width, BLK):
            shape = (spread.shape[0], BLK)
            head = over(iota(shape, 1) + at, head_dim)
            spread[:, at : at + BLK] = jnp.where(
                (iota(shape, 0) & (heads - 1)) == head, 1.0, 0.0
            ).astype(BF16)
        raw = dt_ref[here, :].astype(F32)
        stacked = lambda v: jnp.concatenate([v] * blocks, 0)
        value = jnp.concatenate([raw[:, k * BLK : (k + 1) * BLK] for k in range(blocks)], 0)
        flat = jnp.concatenate(
            [bias_ref[...], rate_ref[...], jnp.zeros((1, BLK - 2 * bias_ref.shape[1]), F32)], 1
        )
        turned = jnp.broadcast_to(flat, (BLK, BLK)).T
        value = value + stacked(turned[here])
        soft = jnp.maximum(value, 0.0) + jnp.log1p(jnp.exp(-jnp.abs(value)))
        shape = value.shape
        position = (
            section * (blocks * BLK) + over(iota(shape, 0), heads) * BLK + iota(shape, 1)
        )
        steps = jnp.where(position < len_ref[0], soft, 0.0)
        log_decay = -steps * stacked(
            turned[bias_ref.shape[1] + group * heads : bias_ref.shape[1] + (group + 1) * heads]
        )
        upper = jnp.where(iota((BLK, BLK), 0) <= iota((BLK, BLK), 1), 1.0, 0.0).astype(BF16)
        cum_log = sum(dot(part, upper) for part in split_three(log_decay))
        owner = over(iota((BLK, BLK), 1), heads)
        for row, full in enumerate((jnp.exp(cum_log), steps * jnp.exp(-cum_log))):
            for part, values in enumerate(split_two(full.T)):
                values = values.astype(F32)
                for block in range(blocks):
                    factors[
                        block, row * BLK : (row + 1) * BLK, part * BLK : (part + 1) * BLK
                    ] = jnp.where(owner == block, values, 0.0).astype(BF16)

    def conv(source, at, size, base, taps, offset):
        now = source[rows, at : at + size].astype(F32)
        cols = slice(base + at, base + at + size)
        joined = jnp.concatenate([behind[:, cols], now], 0)
        total = offset + taps[3:4] * now
        for k in range(3):
            total = total + taps[k : k + 1] * joined[5 + k : 5 + k + BLK]
        behind[:, cols] = now[BLK - 8 :]
        return silu(total)

    causal = iota((BLK, BLK), 0) >= iota((BLK, BLK), 1)
    for sub in range(per_step):
        rows = slice(sub * BLK, (sub + 1) * BLK)
        mixed = conv(
            bc_ref, 0, 2 * state_size, width,
            tap_bc_ref[:, group, :], off_bc_ref[group : group + 1, :],
        )
        c_block = mixed[:, state_size:].astype(BF16)
        b_turned = mixed[:, :state_size].T.astype(BF16)
        c_ref[rows, :] = c_block
        scores = jnp.where(causal, dot(c_block, b_turned), 0.0).astype(BF16)
        left = jnp.concatenate([scores, c_block], 1)
        factor = factors[step * per_step + sub]
        for at in range(0, width, chunk):
            cols = slice(at, at + chunk)
            x_conv = conv(x_ref, at, chunk, 0, tap_x_ref[:, cols], off_x_ref[:, cols])
            scale = dot(factor, spread[:, cols])
            risen = scale[:BLK]
            inner = (x_conv * scale[BLK:]).astype(BF16)
            before = state[:, cols]
            y_local = risen * dot(left, jnp.concatenate([inner, before.astype(BF16)], 0))
            last = risen[BLK - 1 :]
            state[:, cols] = last * (before + dot(b_turned, inner))
            gate = silu(z_ref[rows, cols].astype(F32))
            passed = decay[0:1, cols]
            a_ref[rows, cols] = (y_local * gate).astype(BF16)
            b_ref[rows, cols] = (risen * passed * gate).astype(BF16)
            decay[0:1, cols] = passed * last

    @pl.when(step == pl.num_programs(0) - 1)
    def _():
        t_ref[:BLK] = state[...].astype(BF16)
        row = iota((16, width), 0)
        parts = jnp.zeros((16, width), F32)
        for k, part in enumerate(split_three(decay[0:1, :])):
            parts = jnp.where(row == k, part.astype(F32), parts)
        t_ref[BLK:] = parts.astype(BF16)


def local_part(group, groups, length, x, z, bc, dt, params, received, into):
    bias, rate, tail_x, tail_bc, tap_x, off_x, tap_bc, off_bc = params
    seg_len, channels = x.shape
    blocks = seg_len // BLK
    width = channels // groups
    head_dim = channels // dt.shape[0]
    pair = bc.shape[1] // groups
    body = functools.partial(local_kernel, group=group, blocks=blocks, head_dim=head_dim)
    by_block = lambda size: pl.BlockSpec((LOCAL_ROWS, size), lambda i: (i, group))
    whole = lambda shape: pl.BlockSpec(shape, lambda i: (0,) * len(shape))
    column = lambda size: pl.BlockSpec((size, width), lambda i: (0, group))
    shapes = (
        jax.ShapeDtypeStruct((seg_len, channels), BF16),
        jax.ShapeDtypeStruct((seg_len, channels), BF16),
        jax.ShapeDtypeStruct((seg_len, groups * pair // 2), BF16),
        jax.ShapeDtypeStruct((BLK + 16, width), BF16),
    )
    operands = (
        length, x, z, bc, dt, bias, rate, received, tail_x, tail_bc, tap_x, off_x, tap_bc, off_bc,
    )
    return pl.pallas_call(
        body,
        out_shape=shapes,
        grid=(seg_len // LOCAL_ROWS,),
        in_specs=[
            pl.BlockSpec(memory_space=SMEM),
            by_block(width), by_block(width), by_block(pair),
            whole(dt.shape), whole(bias.shape), whole(rate.shape), whole(received.shape),
            whole(tail_x.shape), whole(tail_bc.shape),
            column(tap_x.shape[0]), column(1), whole(tap_bc.shape), whole(off_bc.shape),
        ] + [pl.BlockSpec(memory_space=pl.ANY)] * len(into),
        out_specs=(
            by_block(width), by_block(width), by_block(pair // 2), whole((BLK + 16, width)),
        ),
        scratch_shapes=[
            VMEM((2 * BLK, width), BF16),
            VMEM((blocks, 2 * BLK, 2 * BLK), BF16),
            VMEM((8, width + pair), F32),
            VMEM((BLK, width), F32),
            VMEM((8, width), F32),
        ],
        input_output_aliases={len(operands) + k: k for k in range(len(into))},
        compiler_params=pltpu.CompilerParams(vmem_limit_bytes=VMEM_LIMIT),
        cost_estimate=pl.CostEstimate(
            flops=2 * seg_len * width * 1024, bytes_accessed=10 * MIB,
            transcendentals=2 * seg_len * width,
        ),
        name="local_blocks",
    )(*operands, *into)


def decay_of(ref, cols):
    rows = ref[BLK : BLK + 16, cols].astype(F32)
    return rows[0:1] + rows[1:2] + rows[2:3]


def moved(ref, cols, cached):
    return decay_of(ref, cols) * cached + ref[:BLK, cols].astype(F32)


def join_kernel(
    group_ref, len_ref, a_ref, b_ref, c_ref, cached_ref, before_ref, gain_ref, *rest, ending
):
    if ending:
        own_ref, mine0_ref, theirs0_ref, mine1_ref, theirs1_ref, _ = rest[:6]
        out_ref, final_ref, start, gated = rest[6:]
    else:
        out_ref, start, gated = rest
    step = pl.program_id(0)
    section = lax.axis_index("section")
    width = a_ref.shape[1]
    chunk = 256

    @pl.when(step == 0)
    def _():
        @pl.when(section == 0)
        def _():
            start[...] = cached_ref[...]

        @pl.when(section == 1)
        def _():
            for at in range(0, width, chunk):
                cols = slice(at, at + chunk)
                start[:, cols] = moved(before_ref, cols, cached_ref[:, cols].astype(F32)).astype(BF16)

    if ending:
        last = pl.num_programs(0) - 1
        orders = ((mine0_ref, theirs0_ref), (theirs1_ref, mine1_ref))
        for place, (early_ref, late_ref) in enumerate(orders):

            @pl.when((step == last) & (section == place))
            def _(early_ref=early_ref, late_ref=late_ref):
                for at in range(0, width, BLK):
                    cols = slice(at, at + BLK)
                    middle = moved(early_ref, cols, own_ref[:, cols].astype(F32))
                    final_ref[cols, :] = moved(late_ref, cols, middle).T

    size = a_ref.shape[0]
    position = (section * pl.num_programs(0) + step) * size + iota((size, 1), 0)
    live = (position < len_ref[0]).astype(F32)
    c_block = c_ref[...]
    squares = jnp.zeros((size, BLK), F32)
    for at in range(0, width, chunk):
        cols = slice(at, at + chunk)
        inter = dot(c_block, start[:, cols])
        value = a_ref[:, cols].astype(F32) + b_ref[:, cols].astype(F32) * inter
        gated[:, cols] = value
        square = value * value
        for k in range(chunk // BLK):
            squares = squares + square[:, k * BLK : (k + 1) * BLK]
    mean = jnp.sum(squares, 1, keepdims=True) * (1.0 / width)
    scale = lax.rsqrt(mean + EPS) * live
    for at in range(0, width, chunk):
        cols = slice(at, at + chunk)
        out_ref[:, cols] = (gated[:, cols] * scale * gain_ref[:, cols]).astype(BF16)


def join_part(group, groups, length, a, b, c, cached, before, gain, ending=()):
    seg_len, channels = a.shape
    width = channels // groups
    by_block = lambda size: pl.BlockSpec((JOIN_ROWS, size), lambda i, at: (i, at[0]))
    whole = lambda shape: pl.BlockSpec(shape, lambda i, at: (0,) * len(shape))
    out_shape = [jax.ShapeDtypeStruct((seg_len, channels), BF16)]
    out_specs = [by_block(width)]
    extra = []
    aliases = {}
    if ending:
        final_shape = (cached.shape[1], cached.shape[0])
        out_shape.append(jax.ShapeDtypeStruct(final_shape, F32))
        out_specs.append(whole(final_shape))
        extra = [whole(v.shape) for v in ending[:-1]] + [pl.BlockSpec(memory_space=pl.ANY)]
        aliases = {8 + len(ending) - 1: 0}
    return pl.pallas_call(
        functools.partial(join_kernel, ending=bool(ending)),
        out_shape=out_shape,
        grid_spec=pltpu.PrefetchScalarGridSpec(
            num_scalar_prefetch=1,
            grid=(seg_len // JOIN_ROWS,),
            in_specs=[
                pl.BlockSpec(memory_space=SMEM),
                by_block(width), by_block(width), by_block(c.shape[1] // groups),
                whole(cached.shape), whole(before.shape),
                pl.BlockSpec((1, width), lambda i, at: (0, at[0])),
            ] + extra,
            out_specs=out_specs,
            scratch_shapes=[VMEM((BLK, width), BF16), VMEM((JOIN_ROWS, width), F32)],
        ),
        input_output_aliases=aliases,
        compiler_params=pltpu.CompilerParams(vmem_limit_bytes=VMEM_LIMIT),
        cost_estimate=pl.CostEstimate(
            flops=2 * seg_len * width * BLK, bytes_accessed=7 * MIB, transcendentals=0
        ),
        name="join_blocks",
    )(group, length, a, b, c, cached, before, gain, *ending)


def body(
    x_in,
    z_in,
    bc_in,
    dt_in,
    tail_x,
    tail_bc,
    conv_w_x,
    conv_b_x,
    conv_w_bc,
    conv_b_bc,
    dt_bias,
    decay_rate,
    norm_gain,
    state_pool,
    block_slots,
    new_len,
):
    section = lax.axis_index("section").astype(jnp.int32)
    section_count = lax.axis_size("section")
    peer_count = lax.axis_size("cache") * lax.axis_size("mp")
    _, seg_len, channels = x_in.shape
    groups = bc_in.shape[2]
    state_size = bc_in.shape[3] // 2
    head_count = dt_in.shape[2]
    head_dim = channels // head_count
    quarter = head_count // section_count
    slots_dev = state_pool.shape[0]
    held = slots_dev // peer_count
    forth, swap = [(0, 1)], [(0, 1), (1, 0)]

    edge = edge_of(x_in[0], bc_in[0])
    received = lax.ppermute(edge, "section", forth)
    outgoing = pack(block_slots, state_pool, edge)
    outgoing, received = lax.optimization_barrier((outgoing, received))
    incoming = lax.all_to_all(
        outgoing.reshape(peer_count, held * head_dim, state_size),
        ("cache", "mp"), split_axis=0, concat_axis=0, tiled=True,
    )

    bc2 = bc_in[0].reshape(seg_len, groups * 2 * state_size)
    params = (
        dt_bias[None], decay_rate[None], tail_x[0], tail_bc[0],
        conv_w_x, conv_b_x[None], conv_w_bc, conv_b_bc,
    )
    shared = (new_len, x_in[0], z_in[0], bc2, dt_in[0].T, params, received)
    a, b, c, mine1 = local_part(1, groups, *shared, ())
    theirs1 = lax.ppermute(mine1, "section", forth)
    a, b, c, mine0 = local_part(0, groups, *shared, (a, b, c))
    theirs0 = lax.ppermute(mine0, "section", swap)

    own = select(
        block_slots, incoming.reshape(peer_count * held, head_dim, state_size), quarter, held
    )
    other = lax.ppermute(own, "section", swap)
    gain = norm_gain[None]
    (gated,) = join_part(section[None], groups, new_len, a, b, c, own, theirs1, gain)
    gated, final = join_part(
        1 - section[None], groups, new_len, a, b, c, other, theirs0, gain,
        (own, mine0, theirs0, mine1, theirs1, gated),
    )
    return (
        gated[None],
        final.reshape(1, 1, 1, quarter, head_dim, state_size),
    )


def solution(mesh):
    in_specs = (
        P("cache", "section", "mp"),
        P("cache", "section", "mp"),
        P("cache", "section", "mp", None),
        P("cache", "section", "mp"),
        P("cache", None, "mp"),
        P("cache", None, "mp", None),
        P(None, "mp"),
        P("mp"),
        P(None, "mp", None),
        P("mp", None),
        P("mp"),
        P("mp"),
        P("mp"),
        P(("section", "cache", "mp"), None, None),
        P(),
        P("cache"),
    )
    out_specs = (P("cache", "section", "mp"), P("cache", "mp", "section", None, None, None))
    return jax.shard_map(body, mesh=mesh, in_specs=in_specs, out_specs=out_specs, check_vma=False)
```

```python
import functools

import jax
import jax.numpy as jnp
from jax import lax
from jax.experimental import pallas as pl
from jax.experimental.pallas import tpu as pltpu
from jax.sharding import PartitionSpec as P

BLK = 128
EPS = 1e-05
JOIN_ROWS = 512
LOCAL_ROWS = 256
MIB = 1 << 20
VMEM_LIMIT = 56 * MIB
EDGE_LIMIT = 63 * MIB
PACK_LIMIT = 61 * MIB
SELECT_LIMIT = 16 * MIB
JOIN_LIMIT = 40 * MIB
F32 = jnp.float32
BF16 = jnp.bfloat16
SMEM = pltpu.SMEM
VMEM = pltpu.VMEM


def dot(a, b):
    return jnp.dot(a, b, preferred_element_type=F32)


def silu(v):
    half = 0.5 * v
    return half * jnp.tanh(half) + half


def split_two(v):
    high = v.astype(BF16)
    return high, (v - high.astype(F32)).astype(BF16)


def split_three(v):
    high = v.astype(BF16)
    rest = v - high.astype(F32)
    mid = rest.astype(BF16)
    return high, mid, (rest - mid.astype(F32)).astype(BF16)


def iota(shape, dim):
    return lax.broadcasted_iota(jnp.int32, shape, dim)


def in_vmem(*values):
    return tuple(pltpu.with_memory_space_constraint(v, pltpu.VMEM) for v in values)


def in_hbm(*values):
    return tuple(pltpu.with_memory_space_constraint(v, pltpu.HBM) for v in values)


def over(v, power_of_two):
    return lax.shift_right_logical(v, jnp.int32(power_of_two.bit_length() - 1))


def edge_kernel(x_ref, bc_ref, edge_ref):
    width = x_ref.shape[1]
    edge_ref[:, :width] = x_ref[...]
    rows = bc_ref[...].astype(F32)
    for group in range(bc_ref.shape[1]):
        at = width + group * bc_ref.shape[2]
        edge_ref[:, at : at + bc_ref.shape[2]] = rows[:, group, :].astype(BF16)


def edge_of(x, bc):
    last = x.shape[0] // 16 - 1
    edge = (16, x.shape[1] + bc.shape[1] * bc.shape[2])
    return pl.pallas_call(
        edge_kernel,
        out_shape=jax.ShapeDtypeStruct(edge, BF16),
        grid=(1,),
        in_specs=[
            pl.BlockSpec((16, x.shape[1]), lambda i: (last, 0)),
            pl.BlockSpec((16,) + bc.shape[1:], lambda i: (last, 0, 0)),
        ],
        out_specs=pl.BlockSpec(edge, lambda i: (0, 0)),
        compiler_params=pltpu.CompilerParams(vmem_limit_bytes=EDGE_LIMIT),
        cost_estimate=pl.CostEstimate(flops=0, bytes_accessed=MIB // 4, transcendentals=0),
        name="edge_rows",
    )(x, bc)


def pack_kernel(
    slots_ref, pool_hbm, edge_hbm, out_ref,
    pool, keys, keys_smem, pool_sems, keys_sem,
):
    step = pl.program_id(0)
    section_count = lax.axis_size("section")
    mp_count = lax.axis_size("mp")
    peer_count = lax.axis_size("cache") * mp_count
    slots_dev = pool.shape[0]
    count = out_ref.shape[0]
    heads = slots_ref.shape[1]
    share = heads // mp_count
    quarter = share // section_count
    held = slots_dev // peer_count
    section = lax.axis_index("section")

    @pl.when(step == 0)
    def _():
        part = slots_dev // pool_sems.shape[0]
        copies = []
        for k in range(pool_sems.shape[0]):
            rows = pl.ds(k * part, part)
            copies.append(pltpu.make_async_copy(pool_hbm.at[rows], pool.at[rows], pool_sems.at[k]))
        for copy in copies:
            copy.start()
        me = lax.axis_index("cache") * mp_count + lax.axis_index("mp")
        slots = slots_ref[...]
        lane = iota(slots.shape, 1)
        mine = lax.rem(lax.div(slots, slots_dev), peer_count) == me
        key = lane * slots_dev + lax.rem(slots, slots_dev)
        first = jnp.where(mine, key, heads * slots_dev)
        last = jnp.where(mine, key, 0)
        shift = 1
        while shift < quarter:
            first = jnp.minimum(first, pltpu.roll(first, heads - shift, 1))
            last = jnp.maximum(last, pltpu.roll(last, heads - shift, 1))
            shift *= 2
        keys[0] = lax.rem(first, slots_dev)
        keys[1] = lax.rem(last, slots_dev)
        listing = pltpu.make_async_copy(keys, keys_smem, keys_sem)
        listing.start()
        listing.wait()
        for copy in copies:
            copy.wait()

    base = step * (count // held)

    def one(i, carry):
        dest = base + i
        row = lax.div(dest, mp_count)
        col = lax.rem(dest, mp_count) * share + section * quarter
        for k in range(held):
            out_ref[held * i + k] = pool[keys_smem[k, row, col]].astype(BF16)
        return carry

    lax.fori_loop(0, count // held, one, 0, unroll=8)


def pack(slots, pool, edge):
    steps = 4
    count = pool.shape[0] // steps
    return pl.pallas_call(
        pack_kernel,
        out_shape=jax.ShapeDtypeStruct(pool.shape, BF16),
        grid=(steps,),
        in_specs=[
            pl.BlockSpec(slots.shape, lambda i: (0, 0)),
            pl.BlockSpec(memory_space=pl.ANY),
            pl.BlockSpec(memory_space=pl.ANY),
        ],
        out_specs=pl.BlockSpec((count,) + pool.shape[1:], lambda i: (i, 0, 0)),
        scratch_shapes=[
            VMEM(pool.shape, F32),
            VMEM((2,) + slots.shape, jnp.int32),
            SMEM((2,) + slots.shape, jnp.int32),
            pltpu.SemaphoreType.DMA((4,)),
            pltpu.SemaphoreType.DMA,
        ],
        compiler_params=pltpu.CompilerParams(vmem_limit_bytes=PACK_LIMIT),
        cost_estimate=pl.CostEstimate(flops=0, bytes_accessed=6 * MIB, transcendentals=0),
        name="pack_states",
    )(slots, pool, edge)


def decay_of(ref, cols):
    rows = ref[BLK : BLK + 16, cols].astype(F32)
    return rows[0:1] + rows[1:2] + rows[2:3]


def moved(ref, cols, cached):
    return decay_of(ref, cols) * cached + ref[:BLK, cols].astype(F32)


def select_kernel(
    slots_ref, incoming_ref, mine_ref, theirs_ref, start_ref, sent_ref, *, slots_dev, held
):
    section_count = lax.axis_size("section")
    mp_count = lax.axis_size("mp")
    peer_count = lax.axis_size("cache") * mp_count
    share = slots_ref.shape[1] // mp_count
    quarter = share // section_count
    row = lax.axis_index("cache")
    at = lax.axis_index("mp") * share + lax.axis_index("section") * quarter
    owners, index = [], []
    for h in range(quarter):
        owner = lax.rem(lax.div(slots_ref[row, at + h], slots_dev), peer_count)
        again = jnp.int32(0)
        for earlier in owners:
            again = jnp.where(earlier == owner, 1, again)
        owners.append(owner)
        index.append(owner * held + again)
    for pair in range(quarter // 2):
        two = jnp.concatenate(
            [incoming_ref[index[2 * pair + k]].astype(F32) for k in range(2)], 0
        )
        cols = slice(pair * BLK, (pair + 1) * BLK)
        cached = two.T

        @pl.when(lax.axis_index("section") == 0)
        def _(cols=cols, cached=cached):
            start_ref[:, cols] = cached.astype(BF16)
            sent_ref[:, cols] = moved(mine_ref, cols, cached).astype(BF16)

        @pl.when(lax.axis_index("section") == 1)
        def _(cols=cols, cached=cached):
            start_ref[:, cols] = moved(theirs_ref, cols, cached).astype(BF16)
            sent_ref[:, cols] = cached.astype(BF16)


def select(slots, incoming, mine, theirs, quarter, held):
    count, head_dim, state_size = incoming.shape
    return pl.pallas_call(
        functools.partial(select_kernel, slots_dev=count, held=held),
        out_shape=[jax.ShapeDtypeStruct((state_size, quarter * head_dim), BF16)] * 2,
        in_specs=[pl.BlockSpec(memory_space=SMEM)] + [pl.BlockSpec(memory_space=VMEM)] * 3,
        out_specs=[pl.BlockSpec(memory_space=VMEM)] * 2,
        compiler_params=pltpu.CompilerParams(vmem_limit_bytes=SELECT_LIMIT),
        cost_estimate=pl.CostEstimate(flops=0, bytes_accessed=3 * MIB, transcendentals=0),
        name="select_states",
    )(slots, incoming, mine, theirs)


def local_kernel(
    group_ref, len_ref, x_ref, z_ref, bc_ref, dt_ref, bias_ref, rate_ref, got_x_ref, got_bc_ref,
    tail_x_ref, tail_bc_ref, tap_x_ref, off_x_ref, tap_bc_ref, off_bc_ref, *rest,
    blocks, head_dim,
):
    a_ref, b_ref, c_ref, t_ref, spread, factors, behind, state, decay = rest[-9:]
    step = pl.program_id(0)
    width = x_ref.shape[1]
    heads = width // head_dim
    state_size = bc_ref.shape[1] // 2
    per_step = x_ref.shape[0] // BLK
    chunk = 256
    is_last = group_ref[0] == 1

    def of_group(low, high):
        return jnp.where(is_last, high, low)

    @pl.when(step == 0)
    def _():
        section = lax.axis_index("section")
        behind[:, :width] = got_x_ref[...].astype(F32)[8:]
        behind[:, width:] = got_bc_ref[...].astype(F32)[8:]

        @pl.when(section == 0)
        def _():
            behind[5:8, :width] = tail_x_ref[...].astype(F32)
            tail = tail_bc_ref[...].astype(F32)
            behind[5:8, width:] = of_group(tail[:, 0, :], tail[:, 1, :])

        state[...] = jnp.zeros_like(state)
        decay[...] = jnp.ones_like(decay)
        for at in range(0, width, BLK):
            shape = (spread.shape[0], BLK)
            head = over(iota(shape, 1) + at, head_dim)
            spread[:, at : at + BLK] = jnp.where(
                (iota(shape, 0) & (heads - 1)) == head, 1.0, 0.0
            ).astype(BF16)
        raw = dt_ref[...].astype(F32)
        stacked = lambda v: jnp.concatenate([v] * blocks, 0)
        value = jnp.concatenate([raw[:, k * BLK : (k + 1) * BLK] for k in range(blocks)], 0)
        flat = jnp.concatenate(
            [bias_ref[...], rate_ref[...], jnp.zeros((1, BLK - 2 * bias_ref.shape[1]), F32)], 1
        )
        turned = jnp.broadcast_to(flat, (BLK, BLK)).T
        column = lambda at: of_group(turned[at : at + heads], turned[at + heads : at + 2 * heads])
        value = value + stacked(column(0))
        soft = jnp.maximum(value, 0.0) + jnp.log1p(jnp.exp(-jnp.abs(value)))
        shape = value.shape
        position = (
            section * (blocks * BLK) + over(iota(shape, 0), heads) * BLK + iota(shape, 1)
        )
        steps = jnp.where(position < len_ref[0], soft, 0.0)
        log_decay = -steps * stacked(column(bias_ref.shape[1]))
        upper = jnp.where(iota((BLK, BLK), 0) <= iota((BLK, BLK), 1), 1.0, 0.0).astype(BF16)
        cum_log = sum(dot(part, upper) for part in split_three(log_decay))
        owner = over(iota((BLK, BLK), 1), heads)
        for row, full in enumerate((jnp.exp(cum_log), steps * jnp.exp(-cum_log))):
            for part, values in enumerate(split_two(full.T)):
                values = values.astype(F32)
                for block in range(blocks):
                    factors[
                        block, row * BLK : (row + 1) * BLK, part * BLK : (part + 1) * BLK
                    ] = jnp.where(owner == block, values, 0.0).astype(BF16)

    def conv(source, at, size, base, taps, offset):
        now = source[rows, at : at + size].astype(F32)
        cols = slice(base + at, base + at + size)
        joined = jnp.concatenate([behind[:, cols], now], 0)
        total = offset + taps[3:4] * now
        for k in range(3):
            total = total + taps[k : k + 1] * joined[5 + k : 5 + k + BLK]
        behind[:, cols] = now[BLK - 8 :]
        return silu(total)

    causal = iota((BLK, BLK), 0) >= iota((BLK, BLK), 1)
    for sub in range(per_step):
        rows = slice(sub * BLK, (sub + 1) * BLK)
        mixed = conv(
            bc_ref, 0, 2 * state_size, width,
            of_group(tap_bc_ref[:, 0, :], tap_bc_ref[:, 1, :]),
            of_group(off_bc_ref[0:1, :], off_bc_ref[1:2, :]),
        )
        c_block = mixed[:, state_size:].astype(BF16)
        b_turned = mixed[:, :state_size].T.astype(BF16)
        c_ref[rows, :] = c_block
        scores = jnp.where(causal, dot(c_block, b_turned), 0.0).astype(BF16)
        left = jnp.concatenate([scores, c_block], 1)
        factor = factors[step * per_step + sub]
        for at in range(0, width, chunk):
            cols = slice(at, at + chunk)
            x_conv = conv(x_ref, at, chunk, 0, tap_x_ref[:, cols], off_x_ref[:, cols])
            scale = dot(factor, spread[:, cols])
            risen = scale[:BLK]
            inner = (x_conv * scale[BLK:]).astype(BF16)
            before = state[:, cols]
            y_local = risen * dot(left, jnp.concatenate([inner, before.astype(BF16)], 0))
            last = risen[BLK - 1 :]
            state[:, cols] = last * (before + dot(b_turned, inner))
            gate = silu(z_ref[rows, cols].astype(F32))
            passed = decay[0:1, cols]
            a_ref[rows, cols] = (y_local * gate).astype(BF16)
            b_ref[rows, cols] = (risen * passed * gate).astype(BF16)
            decay[0:1, cols] = passed * last

    @pl.when(step == pl.num_programs(0) - 1)
    def _():
        t_ref[:BLK] = state[...].astype(BF16)
        row = iota((16, width), 0)
        parts = jnp.zeros((16, width), F32)
        for k, part in enumerate(split_three(decay[0:1, :])):
            parts = jnp.where(row == k, part.astype(F32), parts)
        t_ref[BLK:] = parts.astype(BF16)


def local_part(group, groups, length, x, z, bc, dt, params, received, into):
    bias, rate, tail_x, tail_bc, tap_x, off_x, tap_bc, off_bc = params
    seg_len, channels = x.shape
    blocks = seg_len // BLK
    width = channels // groups
    heads = dt.shape[0] // groups
    pair = bc.shape[1] // groups
    ahead = channels // pair
    body = functools.partial(local_kernel, blocks=blocks, head_dim=width // heads)
    by_block = lambda size: pl.BlockSpec((LOCAL_ROWS, size), lambda i, at: (i, at[0]))
    whole = lambda shape: pl.BlockSpec(shape, lambda i, at: (0,) * len(shape))
    column = lambda size: pl.BlockSpec((size, width), lambda i, at: (0, at[0]))
    shapes = (
        jax.ShapeDtypeStruct((seg_len, channels), BF16),
        jax.ShapeDtypeStruct((seg_len, channels), BF16),
        jax.ShapeDtypeStruct((seg_len, groups * pair // 2), BF16),
        VMEM((BLK + 16, width), BF16),
    )
    operands = (
        group, length, x, z, bc, dt, bias, rate, received, received,
        tail_x, tail_bc, tap_x, off_x, tap_bc, off_bc,
    )
    return pl.pallas_call(
        body,
        out_shape=shapes,
        grid_spec=pltpu.PrefetchScalarGridSpec(
            num_scalar_prefetch=1,
            grid=(seg_len // LOCAL_ROWS,),
            in_specs=[
                pl.BlockSpec(memory_space=SMEM),
                by_block(width), by_block(width), by_block(pair),
                pl.BlockSpec((heads, seg_len), lambda i, at: (at[0], 0)),
                whole(bias.shape), whole(rate.shape),
                column(received.shape[0]),
                pl.BlockSpec((received.shape[0], pair), lambda i, at: (0, ahead + at[0])),
                column(tail_x.shape[0]), whole(tail_bc.shape),
                column(tap_x.shape[0]), column(1), whole(tap_bc.shape), whole(off_bc.shape),
            ] + [pl.BlockSpec(memory_space=pl.ANY)] * len(into),
            out_specs=(
                by_block(width), by_block(width), by_block(pair // 2), whole((BLK + 16, width)),
            ),
            scratch_shapes=[
                VMEM((2 * BLK, width), BF16),
                VMEM((blocks, 2 * BLK, 2 * BLK), BF16),
                VMEM((8, width + pair), F32),
                VMEM((BLK, width), F32),
                VMEM((8, width), F32),
            ],
        ),
        input_output_aliases={len(operands) + k: k for k in range(len(into))},
        compiler_params=pltpu.CompilerParams(vmem_limit_bytes=VMEM_LIMIT),
        cost_estimate=pl.CostEstimate(
            flops=2 * seg_len * width * 1024, bytes_accessed=10 * MIB,
            transcendentals=2 * seg_len * width,
        ),
        name="local_blocks",
    )(*operands, *into)


def join_kernel(group_ref, len_ref, a_ref, b_ref, c_ref, start, gain_ref, *rest, ending):
    if ending:
        sent_ref, mine_ref, theirs_ref, out_ref, final_ref, gated = rest
    else:
        out_ref, gated = rest[1:]
    step = pl.program_id(0)
    section = lax.axis_index("section")
    width = a_ref.shape[1]
    chunk = 256

    if ending:
        for place, (from_ref, late_ref) in enumerate(((sent_ref, theirs_ref), (start, mine_ref))):

            @pl.when((step == 0) & (section == place))
            def _(from_ref=from_ref, late_ref=late_ref):
                for at in range(0, width, BLK):
                    cols = slice(at, at + BLK)
                    final_ref[cols, :] = moved(late_ref, cols, from_ref[:, cols].astype(F32)).T

    size = a_ref.shape[0]
    position = (section * pl.num_programs(0) + step) * size + iota((size, 1), 0)
    live = (position < len_ref[0]).astype(F32)
    c_block = c_ref[...]
    squares = jnp.zeros((size, BLK), F32)
    for at in range(0, width, chunk):
        cols = slice(at, at + chunk)
        inter = dot(c_block, start[:, cols])
        value = a_ref[:, cols].astype(F32) + b_ref[:, cols].astype(F32) * inter
        gated[:, cols] = value
        square = value * value
        for k in range(chunk // BLK):
            squares = squares + square[:, k * BLK : (k + 1) * BLK]
    mean = jnp.sum(squares, 1, keepdims=True) * (1.0 / width)
    scale = lax.rsqrt(mean + EPS) * live
    for at in range(0, width, chunk):
        cols = slice(at, at + chunk)
        out_ref[:, cols] = (gated[:, cols] * scale * gain_ref[:, cols]).astype(BF16)


def join_part(group, groups, length, a, b, c, start, gain, ending=(), into=()):
    seg_len, channels = a.shape
    width = channels // groups
    by_block = lambda size: pl.BlockSpec((JOIN_ROWS, size), lambda i, at: (i, at[0]))
    whole = lambda shape: pl.BlockSpec(shape, lambda i, at: (0,) * len(shape))
    out_shape = [jax.ShapeDtypeStruct((seg_len, channels), BF16)]
    out_specs = [by_block(width)]
    if ending:
        final_shape = (start.shape[1], start.shape[0])
        out_shape.append(jax.ShapeDtypeStruct(final_shape, F32))
        out_specs.append(whole(final_shape))
    return pl.pallas_call(
        functools.partial(join_kernel, ending=bool(ending)),
        out_shape=out_shape,
        grid_spec=pltpu.PrefetchScalarGridSpec(
            num_scalar_prefetch=1,
            grid=(seg_len // JOIN_ROWS,),
            in_specs=[
                pl.BlockSpec(memory_space=SMEM),
                by_block(width), by_block(width), by_block(c.shape[1] // groups),
                pl.BlockSpec(memory_space=VMEM),
                pl.BlockSpec((1, width), lambda i, at: (0, at[0])),
            ]
            + [pl.BlockSpec(memory_space=VMEM)] * len(ending)
            + [pl.BlockSpec(memory_space=pl.ANY)] * len(into),
            out_specs=out_specs,
            scratch_shapes=[VMEM((JOIN_ROWS, width), F32)],
        ),
        input_output_aliases={7: 0} if into else {},
        compiler_params=pltpu.CompilerParams(vmem_limit_bytes=JOIN_LIMIT),
        cost_estimate=pl.CostEstimate(
            flops=2 * seg_len * width * BLK, bytes_accessed=7 * MIB, transcendentals=0
        ),
        name="join_blocks",
    )(group, length, a, b, c, start, gain, *ending, *into)


def body(
    x_in,
    z_in,
    bc_in,
    dt_in,
    tail_x,
    tail_bc,
    conv_w_x,
    conv_b_x,
    conv_w_bc,
    conv_b_bc,
    dt_bias,
    decay_rate,
    norm_gain,
    state_pool,
    block_slots,
    new_len,
):
    section = lax.axis_index("section").astype(jnp.int32)
    section_count = lax.axis_size("section")
    peer_count = lax.axis_size("cache") * lax.axis_size("mp")
    _, seg_len, channels = x_in.shape
    groups = bc_in.shape[2]
    state_size = bc_in.shape[3] // 2
    head_count = dt_in.shape[2]
    head_dim = channels // head_count
    quarter = head_count // section_count
    slots_dev = state_pool.shape[0]
    held = slots_dev // peer_count
    forth, swap = [(0, 1)], [(0, 1), (1, 0)]

    edge = edge_of(x_in[0], bc_in[0])
    received = lax.ppermute(edge, "section", forth)
    outgoing = pack(block_slots, state_pool, edge)
    outgoing, received = lax.optimization_barrier((outgoing, received))
    incoming = lax.all_to_all(
        outgoing.reshape(peer_count, held * head_dim, state_size),
        ("cache", "mp"), split_axis=0, concat_axis=0, tiled=True,
    )

    bc2 = bc_in[0].reshape(seg_len, groups * 2 * state_size)
    params = (
        dt_bias[None], decay_rate[None], tail_x[0], tail_bc[0],
        conv_w_x, conv_b_x[None], conv_w_bc, conv_b_bc,
    )
    shared = (new_len, x_in[0], z_in[0], bc2, dt_in[0].T, params, received)
    far, near = 1 - section[None], section[None]
    a, b, c, leaving = local_part(far, groups, *shared, ())
    theirs = lax.ppermute(leaving, "section", swap)
    a, b, c, mine = local_part(near, groups, *shared, (a, b, c))

    start, sent = select(
        block_slots, incoming.reshape(peer_count * held, head_dim, state_size),
        *in_vmem(mine, theirs), quarter, held,
    )
    other = lax.ppermute(sent, "section", swap)
    gain = norm_gain[None]
    gated, final = join_part(
        near, groups, new_len, *in_hbm(a, b, c), *in_vmem(start), gain,
        in_vmem(sent, mine, theirs),
    )
    (gated,) = join_part(
        far, groups, new_len, *in_hbm(a, b, c), *in_vmem(other), gain, into=in_hbm(gated)
    )
    return (
        gated[None],
        final.reshape(1, 1, 1, quarter, head_dim, state_size),
    )


def solution(mesh):
    in_specs = (
        P("cache", "section", "mp"),
        P("cache", "section", "mp"),
        P("cache", "section", "mp", None),
        P("cache", "section", "mp"),
        P("cache", None, "mp"),
        P("cache", None, "mp", None),
        P(None, "mp"),
        P("mp"),
        P(None, "mp", None),
        P("mp", None),
        P("mp"),
        P("mp"),
        P("mp"),
        P(("section", "cache", "mp"), None, None),
        P(),
        P("cache"),
    )
    out_specs = (P("cache", "section", "mp"), P("cache", "mp", "section", None, None, None))
    return jax.shard_map(body, mesh=mesh, in_specs=in_specs, out_specs=out_specs, check_vma=False)
```

```python
import functools

import jax
import jax.numpy as jnp
from jax import lax
from jax.experimental import pallas as pl
from jax.experimental.pallas import tpu as pltpu
from jax.sharding import PartitionSpec as P

BLK = 128
EPS = 1e-05
JOIN_ROWS = 512
LOCAL_ROWS = 256
MIB = 1 << 20
VMEM_LIMIT = 56 * MIB
EDGE_LIMIT = 63 * MIB
PACK_LIMIT = 61 * MIB
SELECT_LIMIT = 16 * MIB
JOIN_LIMIT = 40 * MIB
F32 = jnp.float32
BF16 = jnp.bfloat16
SMEM = pltpu.SMEM
VMEM = pltpu.VMEM


def dot(a, b):
    return jnp.dot(a, b, preferred_element_type=F32)


def silu(v):
    half = 0.5 * v
    return half * jnp.tanh(half) + half


def split_two(v):
    high = v.astype(BF16)
    return high, (v - high.astype(F32)).astype(BF16)


def split_three(v):
    high = v.astype(BF16)
    rest = v - high.astype(F32)
    mid = rest.astype(BF16)
    return high, mid, (rest - mid.astype(F32)).astype(BF16)


def iota(shape, dim):
    return lax.broadcasted_iota(jnp.int32, shape, dim)


def in_vmem(*values):
    return tuple(pltpu.with_memory_space_constraint(v, pltpu.VMEM) for v in values)


def in_hbm(*values):
    return tuple(pltpu.with_memory_space_constraint(v, pltpu.HBM) for v in values)


def over(v, power_of_two):
    return lax.shift_right_logical(v, jnp.int32(power_of_two.bit_length() - 1))


def edge_kernel(x_ref, bc_ref, edge_ref):
    width = x_ref.shape[1]
    edge_ref[:, :width] = x_ref[...]
    rows = bc_ref[...].astype(F32)
    for group in range(bc_ref.shape[1]):
        at = width + group * bc_ref.shape[2]
        edge_ref[:, at : at + bc_ref.shape[2]] = rows[:, group, :].astype(BF16)


def edge_of(x, bc):
    last = x.shape[0] // 16 - 1
    edge = (16, x.shape[1] + bc.shape[1] * bc.shape[2])
    return pl.pallas_call(
        edge_kernel,
        out_shape=jax.ShapeDtypeStruct(edge, BF16),
        grid=(1,),
        in_specs=[
            pl.BlockSpec((16, x.shape[1]), lambda i: (last, 0)),
            pl.BlockSpec((16,) + bc.shape[1:], lambda i: (last, 0, 0)),
        ],
        out_specs=pl.BlockSpec(edge, lambda i: (0, 0)),
        compiler_params=pltpu.CompilerParams(vmem_limit_bytes=EDGE_LIMIT),
        cost_estimate=pl.CostEstimate(flops=0, bytes_accessed=MIB // 4, transcendentals=0),
        name="edge_rows",
    )(x, bc)


def pack_kernel(
    slots_ref, pool_hbm, edge_hbm, out_ref,
    pool, keys, keys_smem, pool_sems, keys_sem,
):
    step = pl.program_id(0)
    section_count = lax.axis_size("section")
    mp_count = lax.axis_size("mp")
    peer_count = lax.axis_size("cache") * mp_count
    slots_dev = pool.shape[0]
    count = out_ref.shape[0]
    heads = slots_ref.shape[1]
    share = heads // mp_count
    quarter = share // section_count
    held = slots_dev // peer_count
    section = lax.axis_index("section")

    @pl.when(step == 0)
    def _():
        part = slots_dev // pool_sems.shape[0]
        copies = []
        for k in range(pool_sems.shape[0]):
            rows = pl.ds(k * part, part)
            copies.append(pltpu.make_async_copy(pool_hbm.at[rows], pool.at[rows], pool_sems.at[k]))
        for copy in copies:
            copy.start()
        me = lax.axis_index("cache") * mp_count + lax.axis_index("mp")
        slots = slots_ref[...]
        lane = iota(slots.shape, 1)
        mine = lax.rem(lax.div(slots, slots_dev), peer_count) == me
        key = lane * slots_dev + lax.rem(slots, slots_dev)
        first = jnp.where(mine, key, heads * slots_dev)
        last = jnp.where(mine, key, 0)
        shift = 1
        while shift < quarter:
            first = jnp.minimum(first, pltpu.roll(first, heads - shift, 1))
            last = jnp.maximum(last, pltpu.roll(last, heads - shift, 1))
            shift *= 2
        keys[0] = lax.rem(first, slots_dev)
        keys[1] = lax.rem(last, slots_dev)
        listing = pltpu.make_async_copy(keys, keys_smem, keys_sem)
        listing.start()
        listing.wait()
        for copy in copies:
            copy.wait()

    base = step * (count // held)

    def one(i, carry):
        dest = base + i
        row = lax.div(dest, mp_count)
        col = lax.rem(dest, mp_count) * share + section * quarter
        for k in range(held):
            out_ref[held * i + k] = pool[keys_smem[k, row, col]].astype(BF16)
        return carry

    lax.fori_loop(0, count // held, one, 0, unroll=8)


def pack(slots, pool, edge):
    steps = 4
    count = pool.shape[0] // steps
    return pl.pallas_call(
        pack_kernel,
        out_shape=jax.ShapeDtypeStruct(pool.shape, BF16),
        grid=(steps,),
        in_specs=[
            pl.BlockSpec(slots.shape, lambda i: (0, 0)),
            pl.BlockSpec(memory_space=pl.ANY),
            pl.BlockSpec(memory_space=pl.ANY),
        ],
        out_specs=pl.BlockSpec((count,) + pool.shape[1:], lambda i: (i, 0, 0)),
        scratch_shapes=[
            VMEM(pool.shape, F32),
            VMEM((2,) + slots.shape, jnp.int32),
            SMEM((2,) + slots.shape, jnp.int32),
            pltpu.SemaphoreType.DMA((4,)),
            pltpu.SemaphoreType.DMA,
        ],
        compiler_params=pltpu.CompilerParams(vmem_limit_bytes=PACK_LIMIT),
        cost_estimate=pl.CostEstimate(flops=0, bytes_accessed=6 * MIB, transcendentals=0),
        name="pack_states",
    )(slots, pool, edge)


def decay_of(ref, cols):
    rows = ref[BLK : BLK + 16, cols].astype(F32)
    return rows[0:1] + rows[1:2] + rows[2:3]


def moved(ref, cols, cached):
    return decay_of(ref, cols) * cached + ref[:BLK, cols].astype(F32)


def select_kernel(
    slots_ref, incoming_ref, mine_ref, theirs_ref, start_ref, sent_ref, *, slots_dev, held
):
    section_count = lax.axis_size("section")
    mp_count = lax.axis_size("mp")
    peer_count = lax.axis_size("cache") * mp_count
    share = slots_ref.shape[1] // mp_count
    quarter = share // section_count
    row = lax.axis_index("cache")
    at = lax.axis_index("mp") * share + lax.axis_index("section") * quarter
    owners, index = [], []
    for h in range(quarter):
        owner = lax.rem(lax.div(slots_ref[row, at + h], slots_dev), peer_count)
        again = jnp.int32(0)
        for earlier in owners:
            again = jnp.where(earlier == owner, 1, again)
        owners.append(owner)
        index.append(owner * held + again)
    for pair in range(quarter // 2):
        two = jnp.concatenate(
            [incoming_ref[index[2 * pair + k]].astype(F32) for k in range(2)], 0
        )
        cols = slice(pair * BLK, (pair + 1) * BLK)
        cached = two.T

        @pl.when(lax.axis_index("section") == 0)
        def _(cols=cols, cached=cached):
            start_ref[:, cols] = cached.astype(BF16)
            sent_ref[:, cols] = moved(mine_ref, cols, cached).astype(BF16)

        @pl.when(lax.axis_index("section") == 1)
        def _(cols=cols, cached=cached):
            start_ref[:, cols] = moved(theirs_ref, cols, cached).astype(BF16)
            sent_ref[:, cols] = cached.astype(BF16)


def select(slots, incoming, mine, theirs, quarter, held):
    count, head_dim, state_size = incoming.shape
    return pl.pallas_call(
        functools.partial(select_kernel, slots_dev=count, held=held),
        out_shape=[jax.ShapeDtypeStruct((state_size, quarter * head_dim), BF16)] * 2,
        in_specs=[pl.BlockSpec(memory_space=SMEM)] + [pl.BlockSpec(memory_space=VMEM)] * 3,
        out_specs=[pl.BlockSpec(memory_space=VMEM)] * 2,
        compiler_params=pltpu.CompilerParams(vmem_limit_bytes=SELECT_LIMIT),
        cost_estimate=pl.CostEstimate(flops=0, bytes_accessed=3 * MIB, transcendentals=0),
        name="select_states",
    )(slots, incoming, mine, theirs)


def local_kernel(
    group_ref, len_ref, x_ref, z_ref, bc_ref, dt_ref, bias_ref, rate_ref, got_x_ref, got_bc_ref,
    tail_x_ref, tail_bc_ref, tap_x_ref, off_x_ref, tap_bc_ref, off_bc_ref, *rest,
    blocks, head_dim,
):
    a_ref, b_ref, c_ref, t_ref, spread, factors, behind, state, decay = rest[-9:]
    step = pl.program_id(0)
    width = x_ref.shape[1]
    heads = width // head_dim
    state_size = bc_ref.shape[1] // 2
    per_step = x_ref.shape[0] // BLK
    chunk = 256
    is_last = group_ref[0] == 1

    def of_group(low, high):
        return jnp.where(is_last, high, low)

    @pl.when(step == 0)
    def _():
        section = lax.axis_index("section")
        behind[:, :width] = got_x_ref[...].astype(F32)[8:]
        behind[:, width:] = got_bc_ref[...].astype(F32)[8:]

        @pl.when(section == 0)
        def _():
            behind[5:8, :width] = tail_x_ref[...].astype(F32)
            tail = tail_bc_ref[...].astype(F32)
            behind[5:8, width:] = of_group(tail[:, 0, :], tail[:, 1, :])

        state[...] = jnp.zeros_like(state)
        decay[...] = jnp.ones_like(decay)
        for at in range(0, width, BLK):
            shape = (spread.shape[0], BLK)
            head = over(iota(shape, 1) + at, head_dim)
            spread[:, at : at + BLK] = jnp.where(
                (iota(shape, 0) & (heads - 1)) == head, 1.0, 0.0
            ).astype(BF16)
        raw = dt_ref[...].astype(F32)
        stacked = lambda v: jnp.concatenate([v] * blocks, 0)
        value = jnp.concatenate([raw[:, k * BLK : (k + 1) * BLK] for k in range(blocks)], 0)
        flat = jnp.concatenate(
            [bias_ref[...], rate_ref[...], jnp.zeros((1, BLK - 2 * bias_ref.shape[1]), F32)], 1
        )
        turned = jnp.broadcast_to(flat, (BLK, BLK)).T
        column = lambda at: of_group(turned[at : at + heads], turned[at + heads : at + 2 * heads])
        value = value + stacked(column(0))
        soft = jnp.maximum(value, 0.0) + jnp.log1p(jnp.exp(-jnp.abs(value)))
        shape = value.shape
        position = (
            section * (blocks * BLK) + over(iota(shape, 0), heads) * BLK + iota(shape, 1)
        )
        steps = jnp.where(position < len_ref[0], soft, 0.0)
        log_decay = -steps * stacked(column(bias_ref.shape[1]))
        upper = jnp.where(iota((BLK, BLK), 0) <= iota((BLK, BLK), 1), 1.0, 0.0).astype(BF16)
        cum_log = sum(dot(part, upper) for part in split_three(log_decay))
        owner = over(iota((BLK, BLK), 1), heads)
        for row, full in enumerate((jnp.exp(cum_log), steps * jnp.exp(-cum_log))):
            for part, values in enumerate(split_two(full.T)):
                values = values.astype(F32)
                for block in range(blocks):
                    factors[
                        block, row * BLK : (row + 1) * BLK, part * BLK : (part + 1) * BLK
                    ] = jnp.where(owner == block, values, 0.0).astype(BF16)

    def conv(source, at, size, base, taps, offset):
        now = source[rows, at : at + size].astype(F32)
        cols = slice(base + at, base + at + size)
        joined = jnp.concatenate([behind[:, cols], now], 0)
        total = offset + taps[3:4] * now
        for k in range(3):
            total = total + taps[k : k + 1] * joined[5 + k : 5 + k + BLK]
        behind[:, cols] = now[BLK - 8 :]
        return silu(total)

    causal = iota((BLK, BLK), 0) >= iota((BLK, BLK), 1)
    for sub in range(per_step):
        rows = slice(sub * BLK, (sub + 1) * BLK)
        mixed = conv(
            bc_ref, 0, 2 * state_size, width,
            of_group(tap_bc_ref[:, 0, :], tap_bc_ref[:, 1, :]),
            of_group(off_bc_ref[0:1, :], off_bc_ref[1:2, :]),
        )
        c_block = mixed[:, state_size:].astype(BF16)
        b_turned = mixed[:, :state_size].T.astype(BF16)
        c_ref[rows, :] = c_block
        scores = jnp.where(causal, dot(c_block, b_turned), 0.0).astype(BF16)
        left = jnp.concatenate([scores, c_block], 1)
        factor = factors[step * per_step + sub]
        for at in range(0, width, chunk):
            cols = slice(at, at + chunk)
            x_conv = conv(x_ref, at, chunk, 0, tap_x_ref[:, cols], off_x_ref[:, cols])
            scale = dot(factor, spread[:, cols])
            risen = scale[:BLK]
            inner = (x_conv * scale[BLK:]).astype(BF16)
            before = state[:, cols]
            y_local = risen * dot(left, jnp.concatenate([inner, before.astype(BF16)], 0))
            last = risen[BLK - 1 :]
            state[:, cols] = last * (before + dot(b_turned, inner))
            gate = silu(z_ref[rows, cols].astype(F32))
            passed = decay[0:1, cols]
            a_ref[rows, cols] = (y_local * gate).astype(BF16)
            b_ref[rows, cols] = (risen * passed * gate).astype(BF16)
            decay[0:1, cols] = passed * last

    @pl.when(step == pl.num_programs(0) - 1)
    def _():
        t_ref[:BLK] = state[...].astype(BF16)
        row = iota((16, width), 0)
        parts = jnp.zeros((16, width), F32)
        for k, part in enumerate(split_three(decay[0:1, :])):
            parts = jnp.where(row == k, part.astype(F32), parts)
        t_ref[BLK:] = parts.astype(BF16)


def local_part(group, groups, length, x, z, bc, dt, params, received, into):
    bias, rate, tail_x, tail_bc, tap_x, off_x, tap_bc, off_bc = params
    seg_len, channels = x.shape
    blocks = seg_len // BLK
    width = channels // groups
    heads = dt.shape[0] // groups
    pair = bc.shape[1] // groups
    ahead = channels // pair
    body = functools.partial(local_kernel, blocks=blocks, head_dim=width // heads)
    by_block = lambda size: pl.BlockSpec((LOCAL_ROWS, size), lambda i, at: (i, at[0]))
    whole = lambda shape: pl.BlockSpec(shape, lambda i, at: (0,) * len(shape))
    column = lambda size: pl.BlockSpec((size, width), lambda i, at: (0, at[0]))
    shapes = (
        jax.ShapeDtypeStruct((seg_len, channels), BF16),
        jax.ShapeDtypeStruct((seg_len, channels), BF16),
        jax.ShapeDtypeStruct((seg_len, groups * pair // 2), BF16),
        VMEM((BLK + 16, width), BF16),
    )
    operands = (
        group, length, x, z, bc, dt, bias, rate, received, received,
        tail_x, tail_bc, tap_x, off_x, tap_bc, off_bc,
    )
    return pl.pallas_call(
        body,
        out_shape=shapes,
        grid_spec=pltpu.PrefetchScalarGridSpec(
            num_scalar_prefetch=1,
            grid=(seg_len // LOCAL_ROWS,),
            in_specs=[
                pl.BlockSpec(memory_space=SMEM),
                by_block(width), by_block(width), by_block(pair),
                pl.BlockSpec((heads, seg_len), lambda i, at: (at[0], 0)),
                whole(bias.shape), whole(rate.shape),
                column(received.shape[0]),
                pl.BlockSpec((received.shape[0], pair), lambda i, at: (0, ahead + at[0])),
                column(tail_x.shape[0]), whole(tail_bc.shape),
                column(tap_x.shape[0]), column(1), whole(tap_bc.shape), whole(off_bc.shape),
            ] + [pl.BlockSpec(memory_space=pl.ANY)] * len(into),
            out_specs=(
                by_block(width), by_block(width), by_block(pair // 2), whole((BLK + 16, width)),
            ),
            scratch_shapes=[
                VMEM((2 * BLK, width), BF16),
                VMEM((blocks, 2 * BLK, 2 * BLK), BF16),
                VMEM((8, width + pair), F32),
                VMEM((BLK, width), F32),
                VMEM((8, width), F32),
            ],
        ),
        input_output_aliases={len(operands) + k: k for k in range(len(into))},
        compiler_params=pltpu.CompilerParams(vmem_limit_bytes=VMEM_LIMIT),
        cost_estimate=pl.CostEstimate(
            flops=2 * seg_len * width * 1024, bytes_accessed=10 * MIB,
            transcendentals=2 * seg_len * width,
        ),
        name="local_blocks",
    )(*operands, *into)


def join_kernel(group_ref, len_ref, a_ref, b_ref, c_ref, start, gain_ref, *rest, ending):
    if ending:
        sent_ref, mine_ref, theirs_ref, *sources = rest[:6]
        out_ref, final_ref, *handed = rest[6:11]
        gated, sems = rest[11:]
    else:
        out_ref, gated = rest[1:]
    step = pl.program_id(0)
    section = lax.axis_index("section")
    size, width = out_ref.shape
    chunk = 256
    copies = []
    if ending:
        rows = slice(None)
        for at, (source, target) in enumerate(zip(sources, handed)):
            count = target.shape[1]
            cols = pl.ds(pl.multiple_of((1 - section) * count, BLK), count)
            copies.append(pltpu.make_async_copy(source.at[:, cols], target, sems.at[at]))

        @pl.when(step == 0)
        def _():
            for copy in copies:
                copy.start()
    else:
        rows = pl.ds(pl.multiple_of(step * size, size), size)

    if ending:
        for place, (from_ref, late_ref) in enumerate(((sent_ref, theirs_ref), (start, mine_ref))):

            @pl.when((step == 0) & (section == place))
            def _(from_ref=from_ref, late_ref=late_ref):
                for at in range(0, width, BLK):
                    cols = slice(at, at + BLK)
                    final_ref[cols, :] = moved(late_ref, cols, from_ref[:, cols].astype(F32)).T

    position = (section * pl.num_programs(0) + step) * size + iota((size, 1), 0)
    live = (position < len_ref[0]).astype(F32)
    c_block = c_ref[rows, :]
    squares = jnp.zeros((size, BLK), F32)
    for at in range(0, width, chunk):
        cols = slice(at, at + chunk)
        inter = dot(c_block, start[:, cols])
        value = a_ref[rows, cols].astype(F32) + b_ref[rows, cols].astype(F32) * inter
        gated[:, cols] = value
        square = value * value
        for k in range(chunk // BLK):
            squares = squares + square[:, k * BLK : (k + 1) * BLK]
    mean = jnp.sum(squares, 1, keepdims=True) * (1.0 / width)
    scale = lax.rsqrt(mean + EPS) * live
    for at in range(0, width, chunk):
        cols = slice(at, at + chunk)
        out_ref[:, cols] = (gated[:, cols] * scale * gain_ref[:, cols]).astype(BF16)

    if ending:

        @pl.when(step == pl.num_programs(0) - 1)
        def _():
            for copy in copies:
                copy.wait()


def join_part(group, groups, length, a, b, c, start, gain, ending=(), into=()):
    seg_len = a.shape[0]
    state_size, width = start.shape
    channels = groups * width
    by_block = lambda size: pl.BlockSpec((JOIN_ROWS, size), lambda i, at: (i, at[0]))
    kept = pl.BlockSpec(memory_space=VMEM)
    held = [by_block(width), by_block(width), by_block(state_size)] if ending else [kept] * 3
    scratch = [VMEM((JOIN_ROWS, width), F32)]
    extra = [kept] * len(ending)
    whole = lambda shape: pl.BlockSpec(shape, lambda i, at: (0,) * len(shape))
    out_shape = [jax.ShapeDtypeStruct((seg_len, channels), BF16)]
    out_specs = [by_block(width)]
    if ending:
        final_shape = (start.shape[1], start.shape[0])
        out_shape.append(jax.ShapeDtypeStruct(final_shape, F32))
        out_specs.append(whole(final_shape))
        out_shape += [VMEM((seg_len, count), BF16) for count in (width, width, state_size)]
        out_specs += [kept] * 3
        scratch.append(pltpu.SemaphoreType.DMA((3,)))
        extra += [pl.BlockSpec(memory_space=pl.ANY)] * 3
        ending = (*ending, a, b, c)
    return pl.pallas_call(
        functools.partial(join_kernel, ending=bool(ending)),
        out_shape=out_shape,
        grid_spec=pltpu.PrefetchScalarGridSpec(
            num_scalar_prefetch=1,
            grid=(seg_len // JOIN_ROWS,),
            in_specs=[
                pl.BlockSpec(memory_space=SMEM),
                *held,
                kept,
                pl.BlockSpec((1, width), lambda i, at: (0, at[0])),
            ]
            + extra
            + [pl.BlockSpec(memory_space=pl.ANY)] * len(into),
            out_specs=out_specs,
            scratch_shapes=scratch,
        ),
        input_output_aliases={7: 0} if into else {},
        compiler_params=pltpu.CompilerParams(vmem_limit_bytes=JOIN_LIMIT),
        cost_estimate=pl.CostEstimate(
            flops=2 * seg_len * width * BLK, bytes_accessed=7 * MIB, transcendentals=0
        ),
        name="join_blocks",
    )(group, length, a, b, c, start, gain, *ending, *into)


def body(
    x_in,
    z_in,
    bc_in,
    dt_in,
    tail_x,
    tail_bc,
    conv_w_x,
    conv_b_x,
    conv_w_bc,
    conv_b_bc,
    dt_bias,
    decay_rate,
    norm_gain,
    state_pool,
    block_slots,
    new_len,
):
    section = lax.axis_index("section").astype(jnp.int32)
    section_count = lax.axis_size("section")
    peer_count = lax.axis_size("cache") * lax.axis_size("mp")
    _, seg_len, channels = x_in.shape
    groups = bc_in.shape[2]
    state_size = bc_in.shape[3] // 2
    head_count = dt_in.shape[2]
    head_dim = channels // head_count
    quarter = head_count // section_count
    slots_dev = state_pool.shape[0]
    held = slots_dev // peer_count
    forth, swap = [(0, 1)], [(0, 1), (1, 0)]

    edge = edge_of(x_in[0], bc_in[0])
    received = lax.ppermute(edge, "section", forth)
    outgoing = pack(block_slots, state_pool, edge)
    outgoing, received = lax.optimization_barrier((outgoing, received))
    incoming = lax.all_to_all(
        outgoing.reshape(peer_count, held * head_dim, state_size),
        ("cache", "mp"), split_axis=0, concat_axis=0, tiled=True,
    )

    bc2 = bc_in[0].reshape(seg_len, groups * 2 * state_size)
    params = (
        dt_bias[None], decay_rate[None], tail_x[0], tail_bc[0],
        conv_w_x, conv_b_x[None], conv_w_bc, conv_b_bc,
    )
    shared = (new_len, x_in[0], z_in[0], bc2, dt_in[0].T, params, received)
    far, near = 1 - section[None], section[None]
    a, b, c, leaving = local_part(far, groups, *shared, ())
    theirs = lax.ppermute(leaving, "section", swap)
    a, b, c, mine = local_part(near, groups, *shared, (a, b, c))

    start, sent = select(
        block_slots, incoming.reshape(peer_count * held, head_dim, state_size),
        *in_vmem(mine, theirs), quarter, held,
    )
    other = lax.ppermute(sent, "section", swap)
    gain = norm_gain[None]
    gated, final, *parcel = join_part(
        near, groups, new_len, *in_hbm(a, b, c), *in_vmem(start), gain,
        in_vmem(sent, mine, theirs),
    )
    (gated,) = join_part(
        far, groups, new_len, *in_vmem(*parcel), *in_vmem(other), gain, into=in_hbm(gated)
    )
    return (
        gated[None],
        final.reshape(1, 1, 1, quarter, head_dim, state_size),
    )


def solution(mesh):
    in_specs = (
        P("cache", "section", "mp"),
        P("cache", "section", "mp"),
        P("cache", "section", "mp", None),
        P("cache", "section", "mp"),
        P("cache", None, "mp"),
        P("cache", None, "mp", None),
        P(None, "mp"),
        P("mp"),
        P(None, "mp", None),
        P("mp", None),
        P("mp"),
        P("mp"),
        P("mp"),
        P(("section", "cache", "mp"), None, None),
        P(),
        P("cache"),
    )
    out_specs = (P("cache", "section", "mp"), P("cache", "mp", "section", None, None, None))
    return jax.shard_map(body, mesh=mesh, in_specs=in_specs, out_specs=out_specs, check_vma=False)
```
